512 devices in a mesh: chan: 8 (over x, core), row: 8 (over z), col: 8 (over y).
Axes of the slice: x: 4, y: 8, z: 8, core: 2. Of those that a mesh axis runs over, the one named last changes fastest.
Arguments:
- visibility: bfloat16 [64, 1, 2, 2048, 2048], P('chan', None, None, 'row', 'col'), parts along dimension 0
- model: bfloat16 [64, 1, 2, 2048, 2048], P('chan', None, None, 'row', 'col'), parts along dimension 0
- gains_init: float32 [64, 1, 2, 2048], P('chan'), parts along dimension 0, may hold values from 0.1 to 1.9
- antenna_mask: int32 [64, 2048], P('chan'), parts along dimension 0, may hold values 0 or 1
Outputs:
- gains: float32 [64, 1, 2, 2048], P('chan', None, None, 'row'), parts along dimension 0
The draws below stay inside these ranges and needn't reach their ends.
There are 8 independent parts, one for each index of `chan`. The reference program is written for one: setup_inputs(seed, part) draws one part's arguments, and reference() takes and returns one part's arrays. A program takes and returns all parts, laid end to end along the dimension named above; each array names one. Nothing has to cross between parts.
All inputs are finite; a program needn't handle non-finite values.
Results may differ from the reference program's by a relative error of at most 0.0003.
Values sent between devices are 32-bit elements; how exact they have to be, the bound alone decides.
A program may use at most 64 MiB of HBM per device.

```python
import math
import jax
import jax.numpy as jnp
from jax import lax

NA = 2048
POLS = 1
CH = 8
ITERS = 3


def truth_and_model(key, amp_lo, amp_hi, phase_top, scale_top):
    key_model = jax.random.fold_in(key, 101)
    key_amp = jax.random.fold_in(key, 102)
    key_phase = jax.random.fold_in(key, 103)
    key_scale = jax.random.fold_in(key, 104)
    key_place_x = jax.random.fold_in(key, 105)
    key_place_y = jax.random.fold_in(key, 106)
    amp = jnp.exp(jax.random.uniform(key_amp, (CH, POLS, NA), jnp.float32, math.log(amp_lo), math.log(amp_hi)))
    place_x = jax.random.uniform(key_place_x, (CH, POLS, NA), jnp.float32, 0.0, 1.0)
    place_y = jax.random.uniform(key_place_y, (CH, POLS, NA), jnp.float32, 0.0, 1.0)
    jitter = jax.random.uniform(key_phase, (CH, POLS, NA), jnp.float32, -phase_top, phase_top)
    phase = 0.5 * jitter + phase_top * jnp.cos(2.0 * math.pi * place_y)
    scale = jnp.exp(jax.random.uniform(key_scale, (CH, POLS, NA), jnp.float32, 0.0, math.log(scale_top)))
    raw = jax.random.normal(key_model, (CH, POLS, 2, NA, NA), jnp.float32)
    bend = jnp.exp(jnp.cos(2.0 * math.pi * (place_x[:, :, :, None] + place_y[:, :, None, :])))
    model = raw * (scale[:, :, :, None] * scale[:, :, None, :] * bend)[:, :, None]
    return (model, amp * jnp.cos(phase), amp * jnp.sin(phase))


def draw_model(key, part):
    model, g_re, g_im = truth_and_model(key, 0.7, 1.4, 0.8, 1.0)
    return model.astype(jnp.bfloat16)


def draw_visibility(key, part):
    model, g_re, g_im = truth_and_model(key, 0.7, 1.4, 0.8, 1.0)
    key = jax.random.fold_in(key, 7)
    noise = 0.5 * jax.random.normal(key, (CH, POLS, 2, NA, NA), jnp.float32)
    mod_re = model[:, :, 0]
    mod_im = model[:, :, 1]
    left_re = g_re[:, :, :, None]
    left_im = g_im[:, :, :, None]
    right_re = g_re[:, :, None, :]
    right_im = g_im[:, :, None, :]
    part_re = left_re * mod_re - left_im * mod_im
    part_im = left_re * mod_im + left_im * mod_re
    vis_re = part_re * right_re + part_im * right_im
    vis_im = part_im * right_re - part_re * right_im
    return (jnp.stack([vis_re, vis_im], axis=2) + noise).astype(jnp.bfloat16)


def plant(drawn, stream_key, least, high):
    index_at = [jax.random.randint(jax.random.fold_in(stream_key, axis), (), 0, length) for axis, length in enumerate(drawn.shape)]
    widest = drawn.shape.index(max(drawn.shape))
    neighbour = index_at[:widest] + [(index_at[widest] + 1) % drawn.shape[widest]] + index_at[widest + 1:]
    return drawn.at[tuple(index_at)].set(least).at[tuple(neighbour)].set(high)


def setup_inputs(seed: int = 0, part: int = 0) -> dict:
    streams_of = jax.random.split(jax.random.key(seed), 5)
    part_splits = jax.random.split(jax.random.fold_in(streams_of[4], part), 5)
    return {
        "visibility": draw_visibility(jax.random.fold_in(jax.random.fold_in(streams_of[4], part), 71), part),
        "model": draw_model(jax.random.fold_in(jax.random.fold_in(streams_of[4], part), 71), part),
        "gains_init": jnp.clip(1.0 + 0.18 * jax.random.normal(part_splits[2], (CH, POLS, 2, NA), jnp.float32), 0.1, 1.9),
        "antenna_mask": plant((jax.random.randint(part_splits[3], (CH, NA), 0, 8) < 7).astype(jnp.int32), jax.random.fold_in(part_splits[3], 1), 0, 1),
    }


def solve_channel(items):
    visibility, model, gains_init, antenna_mask = items
    vis_re = visibility[:, 0].astype(jnp.float32)
    vis_im = visibility[:, 1].astype(jnp.float32)
    mod_re = model[:, 0].astype(jnp.float32)
    mod_im = model[:, 1].astype(jnp.float32)
    mask_f = antenna_mask.astype(jnp.float32)
    idx = lax.iota(jnp.int32, NA)
    off_diag = (idx[:, None] != idx[None, :]).astype(jnp.float32)
    weight = (mask_f[:, None] * mask_f[None, :] * off_diag)[None]
    gains = gains_init.astype(jnp.float32)
    for step in range(ITERS):
        g_re = gains[:, 0][:, None, :]
        g_im = gains[:, 1][:, None, :]
        z_re = mod_re * g_re + mod_im * g_im
        z_im = mod_im * g_re - mod_re * g_im
        num_re = jnp.sum(weight * (z_re * vis_re + z_im * vis_im), axis=-1)
        num_im = jnp.sum(weight * (z_re * vis_im - z_im * vis_re), axis=-1)
        den = jnp.sum(weight * (z_re * z_re + z_im * z_im), axis=-1)
        scale = mask_f[None] / jnp.maximum(den, 1.0)
        keep = 1.0 - mask_f[None]
        new_re = num_re * scale + keep * gains[:, 0]
        new_im = num_im * scale + keep * gains[:, 1]
        fresh = jnp.stack([new_re, new_im], axis=1)
        if step % 2 == 1:
            gains = 0.5 * (fresh + gains)
        else:
            gains = fresh
    return gains


def reference(visibility, model, gains_init, antenna_mask):
    return lax.map(solve_channel, (visibility, model, gains_init, antenna_mask))
```

```python
import functools

import jax
import jax.numpy as jnp
from jax import lax
from jax.experimental import pallas as pl
from jax.experimental.pallas import tpu as pltpu
from jax.sharding import PartitionSpec as P

ITERS = 3
MESH = pl.DeviceIdType.MESH
SHRINK = 2.0**-8
HUGE = 2.0**60
HUGE_SHRINK = 2.0**-65
LOWER = 2.0**-4
HUGE_GROW = 2.0**126
LEAST = SHRINK * LOWER
CHUNK = 32


def split(x):
    high = x.astype(jnp.bfloat16).astype(jnp.float32)
    return high, x - high


def stack_bf16(parts):
    return jnp.concatenate(parts, axis=0).astype(jnp.bfloat16)


def dot_nt(x, y):
    return lax.dot_general(x, y, (((1,), (1,)), ((), ())), preferred_element_type=jnp.float32)


def kernel(
    n, vis, mod, gin, mask, out,
    vbuf, mbuf, abuf, bbuf, weight, gcol, gown, mcol, mrow,
    part, recv, gsend, xbuf,
    in_sem, small_sem, send1, recv1, send2, recv2, send3, recv3, self_sem,
):
    row = lax.axis_index("row")
    col = lax.axis_index("col")
    wide = weight.shape[1]
    diag = row == col

    def loads(k):
        return (
            pltpu.make_async_copy(vis.at[k], vbuf.at[k], in_sem.at[0, k]),
            pltpu.make_async_copy(mod.at[k], mbuf.at[k], in_sem.at[1, k]),
        )

    row_at = pl.ds(pl.multiple_of(row * wide, wide), wide)
    col_at = pl.ds(pl.multiple_of(col * wide, wide), wide)
    small = (
        pltpu.make_async_copy(gin.at[:, :, col_at], gcol, small_sem.at[0]),
        pltpu.make_async_copy(mask.at[:, col_at], mcol, small_sem.at[1]),
        pltpu.make_async_copy(mask.at[:, row_at], mrow, small_sem.at[2]),
        pltpu.make_async_copy(gin.at[col, :, row_at], gown, small_sem.at[3]),
    )
    for step in range(1, n + 1):
        for copy in loads(lax.rem(col + step, n)):
            copy.start()
        if step == 1:
            for copy in small:
                copy.start()

    barrier = pltpu.get_barrier_semaphore()
    for step in range(1, n):
        pl.semaphore_signal(barrier, inc=1, device_id={"col": lax.rem(col + step, n)}, device_id_type=MESH)
    for step in range(n):
        peer = {"row": col, "col": lax.rem(col + step, n)}
        if step == 0:
            @pl.when(jnp.logical_not(diag))
            def _():
                pl.semaphore_signal(barrier, inc=1, device_id=peer, device_id_type=MESH)
        else:
            pl.semaphore_signal(barrier, inc=1, device_id=peer, device_id_type=MESH)

    row_ids = lax.broadcasted_iota(jnp.int32, weight.shape, 0) + row * wide
    col_ids = lax.broadcasted_iota(jnp.int32, weight.shape, 1) + col * wide
    weight[...] = jnp.where(row_ids == col_ids, 0.0, SHRINK)

    for copy in small:
        copy.wait()
    xbuf[0] = gcol[...] * mcol[...].astype(jnp.float32)[:, None, :]

    even = lax.rem(lax.broadcasted_iota(jnp.int32, (8, wide), 0), 2) == 0
    top = lax.broadcasted_iota(jnp.int32, (4, wide), 0) < 2

    def prepare(k):
        for copy in loads(k):
            copy.wait()
        for at in range(0, wide, CHUNK):
            rows = pl.ds(at, CHUNK)
            scale = weight[rows]
            m_re = mbuf[k, 0, rows].astype(jnp.float32)
            m_im = mbuf[k, 1, rows].astype(jnp.float32)
            v_re = vbuf[k, 0, rows].astype(jnp.float32)
            v_im = vbuf[k, 1, rows].astype(jnp.float32)
            s_re = m_re * scale
            s_im = m_im * scale
            for place, value in enumerate((s_re * v_re + s_im * v_im, s_re * v_im - s_im * v_re)):
                high = value.astype(jnp.bfloat16)
                abuf[k, rows, (2 * place) * wide:(2 * place + 1) * wide] = high
                abuf[k, rows, (2 * place + 1) * wide:(2 * place + 2) * wide] = (value - high.astype(jnp.float32)).astype(jnp.bfloat16)
            value = s_re * m_re + s_im * m_im
            high = value.astype(jnp.bfloat16)
            bbuf[k, rows, 0:wide] = high
            bbuf[k, rows, wide:2 * wide] = (value - high.astype(jnp.float32)).astype(jnp.bfloat16)

    def multiply(it, k):
        x_re = jnp.broadcast_to(xbuf[it, k, 0:1, :], (8, wide))
        x_im = jnp.broadcast_to(xbuf[it, k, 1:2, :], (8, wide))
        by_re = stack_bf16(split(jnp.where(even, x_re, x_im)))
        by_im = stack_bf16(split(jnp.where(even, -x_im, x_re)))
        huge = jnp.maximum(jnp.abs(x_re), jnp.abs(x_im)) > HUGE
        down = jnp.where(huge, HUGE_SHRINK, 1.0)
        square = (x_re * down) * (x_re * down) + (x_im * down) * (x_im * down)
        by_b = stack_bf16(split(jnp.where(huge, 0.0, square)) + split(jnp.where(huge, square, 0.0)))
        num = dot_nt(jnp.concatenate([by_re, by_re, by_im, by_im], axis=1), abuf[k])
        den = dot_nt(jnp.concatenate([by_b, by_b], axis=1), bbuf[k])
        num = (num[0:8] + num[8:16]) * LOWER
        den = (den[0:8] + den[8:16]) * LOWER + (den[16:24] + den[24:32]) * HUGE_GROW
        part[it, k] = jnp.where(top, num[0:4], den[0:4])

    def send_part(it, step):
        k = lax.rem(col + step, n)
        pltpu.make_async_remote_copy(
            src_ref=part.at[it, k], dst_ref=recv.at[it, step - 1],
            send_sem=send1.at[it], recv_sem=recv1.at[it],
            device_id={"col": k}, device_id_type=MESH,
        ).start()

    def wait_bytes(ref, sem):
        pltpu.make_async_copy(ref, ref, sem).wait()

    for it in range(ITERS):
        if it == 0:
            first = lax.rem(col + 1, n)
            prepare(first)
            multiply(0, first)
            pl.semaphore_wait(barrier, 2 * n - 1 - diag.astype(jnp.int32))
            send_part(0, 1)

            @pl.loop(2, n)
            def _(step):
                k = lax.rem(col + step, n)
                prepare(k)
                multiply(0, k)
                send_part(0, step)

            prepare(col)
            multiply(0, col)
        else:
            wait_bytes(xbuf.at[it], recv2.at[it - 1])

            @pl.loop(1, n)
            def _(step):
                multiply(it, lax.rem(col + step, n))
                send_part(it, step)

            multiply(it, col)

        wait_bytes(recv.at[it], recv1.at[it])
        total = part[it, col]
        for step in range(n - 1):
            total = total + recv[it, step]
        old = gown[...]
        own_mask = mrow[pl.ds(col, 1), :].astype(jnp.float32)
        fresh = total[0:2] / jnp.maximum(total[2:4], LEAST)
        fresh = jnp.where(own_mask > 0.0, fresh, old)
        if it % 2 == 1:
            fresh = 0.5 * (fresh + old)
        if it < ITERS - 1:
            gown[...] = fresh
            gsend[it] = fresh * own_mask
            for step in range(n):
                peer = {"row": lax.rem(row + step, n), "col": row}

                def remote(step=step, peer=peer):
                    pltpu.make_async_remote_copy(
                        src_ref=gsend.at[it], dst_ref=xbuf.at[it + 1, col],
                        send_sem=send2.at[it, min(step, 1)], recv_sem=recv2.at[it],
                        device_id=peer, device_id_type=MESH,
                    ).start()

                if step == 0:
                    pl.when(jnp.logical_not(diag))(remote)

                    @pl.when(diag)
                    def _():
                        pltpu.make_async_copy(gsend.at[it], xbuf.at[it + 1, col], recv2.at[it]).start()
                else:
                    remote()
        else:
            gsend[it] = fresh
            for step in range(1, n):
                pltpu.make_async_remote_copy(
                    src_ref=gsend.at[it], dst_ref=out.at[col],
                    send_sem=send3, recv_sem=recv3,
                    device_id={"col": lax.rem(col + step, n)}, device_id_type=MESH,
                ).start()
            own = pltpu.make_async_copy(gsend.at[it], out.at[col], self_sem)
            own.start()
            own.wait()

    for it in range(ITERS):
        wait_bytes(recv.at[it], send1.at[it])
        if it < ITERS - 1:
            wait_bytes(xbuf.at[it + 1, 0:n - 1], send2.at[it, 1])

            @pl.when(jnp.logical_not(diag))
            def _():
                wait_bytes(gsend.at[it], send2.at[it, 0])
    wait_bytes(xbuf.at[0, 0:n - 1], send3)
    wait_bytes(xbuf.at[0, 0:n - 1], recv3)


def per_device(n, visibility, model, gains_init, antenna_mask):
    ch, _, _, rows, wide = visibility.shape
    f32, bf16 = jnp.float32, jnp.bfloat16
    hbm = pl.BlockSpec(memory_space=pltpu.HBM)
    dma = pltpu.SemaphoreType.DMA
    gains = pl.pallas_call(
        functools.partial(kernel, n),
        out_shape=jax.ShapeDtypeStruct((ch, 2, wide), f32),
        in_specs=[hbm] * 4,
        out_specs=hbm,
        scratch_shapes=[
            pltpu.VMEM((ch, 2, rows, wide), bf16),
            pltpu.VMEM((ch, 2, rows, wide), bf16),
            pltpu.VMEM((ch, rows, 4 * wide), bf16),
            pltpu.VMEM((ch, rows, 2 * wide), bf16),
            pltpu.VMEM((rows, wide), f32),
            pltpu.VMEM((ch, 2, wide), f32),
            pltpu.VMEM((2, wide), f32),
            pltpu.VMEM((ch, wide), jnp.int32),
            pltpu.VMEM((ch, wide), jnp.int32),
            pltpu.VMEM((ITERS, ch, 4, wide), f32),
            pltpu.VMEM((ITERS, n - 1, 4, wide), f32),
            pltpu.VMEM((ITERS, 2, wide), f32),
            pltpu.VMEM((ITERS, ch, 2, wide), f32),
            dma((2, ch)),
            dma((4,)),
            dma((ITERS,)),
            dma((ITERS,)),
            dma((ITERS - 1, 2)),
            dma((ITERS - 1,)),
            dma,
            dma,
            dma,
        ],
        compiler_params=pltpu.CompilerParams(
            collective_id=0, has_side_effects=True, vmem_limit_bytes=60 * 2**20
        ),
        cost_estimate=pl.CostEstimate(flops=2 * 48 * 16 * 256 * 256 * 3, bytes_accessed=4 * 2**20, transcendentals=0),
    )(
        visibility.reshape(ch, 2, rows, wide),
        model.reshape(ch, 2, rows, wide),
        gains_init.reshape(ch, 2, gains_init.shape[3]),
        antenna_mask,
    )
    return gains.reshape(ch, 1, 2, wide)


def solution(mesh):
    n = mesh.shape["col"]
    assert mesh.shape["row"] == n
    return jax.shard_map(
        functools.partial(per_device, n),
        mesh=mesh,
        in_specs=(
            P("chan", None, None, "row", "col"),
            P("chan", None, None, "row", "col"),
            P("chan", None, None, None),
            P("chan", None),
        ),
        out_specs=P("chan", None, None, "row"),
        check_vma=False,
    )
```

```python
import functools

import jax
import jax.numpy as jnp
from jax import lax
from jax.experimental import pallas as pl
from jax.experimental.pallas import tpu as pltpu
from jax.sharding import PartitionSpec as P

ITERS = 3
MESH = pl.DeviceIdType.MESH
SHRINK = 2.0**-8
HUGE = 2.0**60
HUGE_SHRINK = 2.0**-65
LOWER = 2.0**-4
HUGE_GROW = 2.0**126
LEAST = SHRINK * LOWER
CHUNK = 32


def split(x):
    high = x.astype(jnp.bfloat16).astype(jnp.float32)
    return high, x - high


def stack_bf16(parts):
    return jnp.concatenate(parts, axis=0).astype(jnp.bfloat16)


def dot_nt(x, y):
    return lax.dot_general(x, y, (((1,), (1,)), ((), ())), preferred_element_type=jnp.float32)


def farthest_first(n):
    return sorted(range(1, n), key=lambda step: -min(step, n - step))


def kernel(
    n, vis, mod, gin, mask, out,
    vbuf, mbuf, abuf, bbuf, weight, gcol, grow, mcol, mrow, old, sums, xbuf, final,
    in_sem, small_sem, sum_send, sum_recv, x_send, x_recv, out_sem,
):
    row = lax.axis_index("row")
    col = lax.axis_index("col")
    ch, wide = mcol.shape
    diag = row == col

    def loads(k):
        return (
            pltpu.make_async_copy(vis.at[k], vbuf.at[k], in_sem.at[0, k]),
            pltpu.make_async_copy(mod.at[k], mbuf.at[k], in_sem.at[1, k]),
        )

    row_at = pl.ds(pl.multiple_of(row * wide, wide), wide)
    col_at = pl.ds(pl.multiple_of(col * wide, wide), wide)
    small = (
        pltpu.make_async_copy(gin.at[:, :, col_at], gcol, small_sem.at[0]),
        pltpu.make_async_copy(mask.at[:, col_at], mcol, small_sem.at[1]),
        pltpu.make_async_copy(mask.at[:, row_at], mrow, small_sem.at[2]),
        pltpu.make_async_copy(gin.at[:, :, row_at], grow, small_sem.at[3]),
    )
    for k in range(ch):
        for copy in loads(k):
            copy.start()
        if k == 0:
            for copy in small:
                copy.start()

    barrier = pltpu.get_barrier_semaphore()
    for step in range(1, n):
        pl.semaphore_signal(barrier, inc=1, device_id={"col": lax.rem(col + step, n)}, device_id_type=MESH)

    @pl.when(jnp.logical_not(diag))
    def _():
        pl.semaphore_signal(barrier, inc=1, device_id={"row": col}, device_id_type=MESH)

    row_ids = lax.broadcasted_iota(jnp.int32, weight.shape, 0) + row * wide
    col_ids = lax.broadcasted_iota(jnp.int32, weight.shape, 1) + col * wide
    weight[...] = jnp.where(row_ids == col_ids, 0.0, SHRINK)

    for copy in small:
        copy.wait()
    col_mask = mcol[...].astype(jnp.float32)
    for part in range(2):
        xbuf[0, part] = gcol[:, part, :] * col_mask
        old[part] = grow[:, part, :]

    channel = lax.broadcasted_iota(jnp.int32, (ch, wide), 0)

    def prepare(k):
        for copy in loads(k):
            copy.wait()
        for at in range(0, wide, CHUNK):
            rows = pl.ds(at, CHUNK)
            scale = weight[rows]
            m_re = mbuf[k, 0, rows].astype(jnp.float32)
            m_im = mbuf[k, 1, rows].astype(jnp.float32)
            v_re = vbuf[k, 0, rows].astype(jnp.float32)
            v_im = vbuf[k, 1, rows].astype(jnp.float32)
            s_re = m_re * scale
            s_im = m_im * scale
            for place, value in enumerate((s_re * v_re + s_im * v_im, s_re * v_im - s_im * v_re)):
                high = value.astype(jnp.bfloat16)
                abuf[k, rows, (2 * place) * wide:(2 * place + 1) * wide] = high
                abuf[k, rows, (2 * place + 1) * wide:(2 * place + 2) * wide] = (value - high.astype(jnp.float32)).astype(jnp.bfloat16)
            value = s_re * m_re + s_im * m_im
            high = value.astype(jnp.bfloat16)
            bbuf[k, rows, 0:wide] = high
            bbuf[k, rows, wide:2 * wide] = (value - high.astype(jnp.float32)).astype(jnp.bfloat16)

    def multiply(it):
        x_re = xbuf[it, 0]
        x_im = xbuf[it, 1]
        re = split(x_re)
        im = split(x_im)
        by_re = stack_bf16(re + im)
        by_im = stack_bf16((-im[0], -im[1]) + re)
        huge = jnp.maximum(jnp.abs(x_re), jnp.abs(x_im)) > HUGE
        down = jnp.where(huge, HUGE_SHRINK, 1.0)
        square = (x_re * down) * (x_re * down) + (x_im * down) * (x_im * down)
        by_b = stack_bf16(split(jnp.where(huge, 0.0, square)) + split(jnp.where(huge, square, 0.0)))
        by_a = jnp.concatenate([by_re, by_re, by_im, by_im], axis=1)
        by_b = jnp.concatenate([by_b, by_b], axis=1)
        num_re = num_im = den = jnp.zeros((ch, wide), jnp.float32)
        for k in range(ch):
            num = dot_nt(by_a, abuf[k])
            sq = dot_nt(by_b, bbuf[k])
            here = channel == k
            num_re = jnp.where(here, num[0:ch] + num[ch:2 * ch], num_re)
            num_im = jnp.where(here, num[2 * ch:3 * ch] + num[3 * ch:4 * ch], num_im)
            den = jnp.where(here, (sq[0:ch] + sq[ch:2 * ch]) * LOWER + (sq[2 * ch:3 * ch] + sq[3 * ch:4 * ch]) * HUGE_GROW, den)
        sums[it, col, 0] = num_re * LOWER
        sums[it, col, 1] = num_im * LOWER
        sums[it, col, 2] = den

    def sum_to(it, peer):
        return pltpu.make_async_remote_copy(
            src_ref=sums.at[it, col], dst_ref=sums.at[it, col],
            send_sem=sum_send.at[it], recv_sem=sum_recv.at[it],
            device_id={"col": peer}, device_id_type=MESH,
        )

    def wait_bytes(ref, sem):
        pltpu.make_async_copy(ref, ref, sem).wait()

    def update(it):
        wait_bytes(sums.at[it, 0:n - 1], sum_recv.at[it])
        usable = mrow[...] > 0
        total = [sums[it, 0, place] for place in range(3)]
        for peer in range(1, n):
            for place in range(3):
                total[place] = total[place] + sums[it, peer, place]
        least = jnp.maximum(total[2], LEAST)
        return [jnp.where(usable, total[part] / least, grow[:, part, :]) for part in range(2)], usable

    for it in range(ITERS):
        if it == 0:
            @pl.loop(0, ch)
            def _(k):
                prepare(k)
        else:
            @pl.when(jnp.logical_not(diag))
            def _():
                wait_bytes(xbuf.at[it], x_recv.at[it - 1])
        multiply(it)
        if it == 0:
            pl.semaphore_wait(barrier, n - 1 + (n - 1) * diag.astype(jnp.int32))
        if it < ITERS - 1:
            @pl.when(jnp.logical_not(diag))
            def _():
                sum_to(it, row).start()

            @pl.when(diag)
            def _():
                fresh, usable = update(it)
                for part in range(2):
                    value = fresh[part]
                    if it % 2 == 1:
                        value = jnp.where(usable, 0.5 * (value + old[part]), value)
                    old[part] = value
                    xbuf[it + 1, part] = jnp.where(usable, value, 0.0)
                for step in farthest_first(n):
                    pltpu.make_async_remote_copy(
                        src_ref=xbuf.at[it + 1], dst_ref=xbuf.at[it + 1],
                        send_sem=x_send.at[it], recv_sem=x_recv.at[it],
                        device_id={"row": lax.rem(row + step, n)}, device_id_type=MESH,
                    ).start()
        else:
            for step in farthest_first(n):
                sum_to(it, lax.rem(col + step, n)).start()
            fresh, usable = update(it)
            for part in range(2):
                final[:, part, :] = fresh[part]
            done = pltpu.make_async_copy(final, out, out_sem)
            done.start()
            done.wait()

    for it in range(ITERS - 1):
        @pl.when(jnp.logical_not(diag))
        def _():
            wait_bytes(sums.at[it, 0], sum_send.at[it])

        @pl.when(diag)
        def _():
            wait_bytes(sums.at[0, 0:n - 1, 0:2], x_send.at[it])
    wait_bytes(sums.at[0, 0:n - 1], sum_send.at[ITERS - 1])


def per_device(n, visibility, model, gains_init, antenna_mask):
    assert ITERS % 2 == 1
    ch, _, _, rows, wide = visibility.shape
    f32, bf16 = jnp.float32, jnp.bfloat16
    hbm = pl.BlockSpec(memory_space=pltpu.HBM)
    dma = pltpu.SemaphoreType.DMA
    gains = pl.pallas_call(
        functools.partial(kernel, n),
        out_shape=jax.ShapeDtypeStruct((ch, 2, wide), f32),
        in_specs=[hbm] * 4,
        out_specs=hbm,
        scratch_shapes=[
            pltpu.VMEM((ch, 2, rows, wide), bf16),
            pltpu.VMEM((ch, 2, rows, wide), bf16),
            pltpu.VMEM((ch, rows, 4 * wide), bf16),
            pltpu.VMEM((ch, rows, 2 * wide), bf16),
            pltpu.VMEM((rows, wide), f32),
            pltpu.VMEM((ch, 2, wide), f32),
            pltpu.VMEM((ch, 2, wide), f32),
            pltpu.VMEM((ch, wide), jnp.int32),
            pltpu.VMEM((ch, wide), jnp.int32),
            pltpu.VMEM((2, ch, wide), f32),
            pltpu.VMEM((ITERS, n, 3, ch, wide), f32),
            pltpu.VMEM((ITERS, 2, ch, wide), f32),
            pltpu.VMEM((ch, 2, wide), f32),
            dma((2, ch)),
            dma((4,)),
            dma((ITERS,)),
            dma((ITERS,)),
            dma((ITERS - 1,)),
            dma((ITERS - 1,)),
            dma,
        ],
        compiler_params=pltpu.CompilerParams(
            collective_id=0, has_side_effects=True, vmem_limit_bytes=60 * 2**20
        ),
        cost_estimate=pl.CostEstimate(flops=2 * 48 * 32 * 256 * 256 * 3, bytes_accessed=4 * 2**20, transcendentals=0),
    )(
        visibility.reshape(ch, 2, rows, wide),
        model.reshape(ch, 2, rows, wide),
        gains_init.reshape(ch, 2, gains_init.shape[3]),
        antenna_mask,
    )
    return gains.reshape(ch, 1, 2, wide)


def solution(mesh):
    n = mesh.shape["col"]
    assert mesh.shape["row"] == n
    return jax.shard_map(
        functools.partial(per_device, n),
        mesh=mesh,
        in_specs=(
            P("chan", None, None, "row", "col"),
            P("chan", None, None, "row", "col"),
            P("chan", None, None, None),
            P("chan", None),
        ),
        out_specs=P("chan", None, None, "row"),
        check_vma=False,
    )
```

```python
import functools

import jax
import jax.numpy as jnp
from jax import lax
from jax.experimental import pallas as pl
from jax.experimental.pallas import tpu as pltpu
from jax.sharding import PartitionSpec as P

ITERS = 3
HALVES = 2
CORES = 2
MESH = pl.DeviceIdType.MESH
SHRINK = 2.0**-5
HUGE = 2.0**60
HUGE_SHRINK = 2.0**-65
DEN_LOWER = 2.0**-4
HUGE_GROW = 2.0**126
NUM_LOWER = SHRINK * DEN_LOWER
LEAST = SHRINK * NUM_LOWER
CHUNK = 32


def split(x):
    high = x.astype(jnp.bfloat16).astype(jnp.float32)
    return high, x - high


def stack_bf16(x):
    return jnp.concatenate(split(x), axis=0).astype(jnp.bfloat16)


def dot(x, y, side):
    return lax.dot_general(x, y, (((1,), (side,)), ((), ())), preferred_element_type=jnp.float32)


def farthest_first(n):
    return sorted(range(1, n), key=lambda step: -min(step, n - step))


def kernel(
    n, vis, mod, gin, mask, out,
    vbuf, mbuf, abuf, bbuf, aflip, bflip, weight, gcol, grow, mcol, mrow, old,
    mine, sums, fresh, arrived, last, final,
    in_sem, small_sem, sum_send, sum_recv, x_send, x_recv, last_send, last_recv, out_sem,
):
    chan = lax.axis_index("chan")
    row = lax.axis_index("row")
    col = lax.axis_index("col")
    ch, wide = mcol.shape
    half = ch // HALVES
    core = lax.rem(chan, CORES)
    upper = chan - core + 1
    diag = row == col
    owner = jnp.logical_and(diag, core == 1)
    other = jnp.logical_not(owner)
    column_owner = {"chan": upper, "row": col, "col": col}
    row_owner = {"chan": upper, "row": row, "col": row}

    def loads(k):
        return (
            pltpu.make_async_copy(vis.at[k], vbuf.at[k], in_sem.at[0, k]),
            pltpu.make_async_copy(mod.at[k], mbuf.at[k], in_sem.at[1, k]),
        )

    row_at = pl.ds(pl.multiple_of(row * wide, wide), wide)
    col_at = pl.ds(pl.multiple_of(col * wide, wide), wide)
    small = (
        pltpu.make_async_copy(gin.at[:, :, col_at], gcol, small_sem.at[0]),
        pltpu.make_async_copy(mask.at[:, col_at], mcol, small_sem.at[1]),
        pltpu.make_async_copy(mask.at[:, row_at], mrow, small_sem.at[2]),
        pltpu.make_async_copy(gin.at[:, :, row_at], grow, small_sem.at[3]),
    )
    for k in range(ch):
        for copy in loads(k):
            copy.start()
        if k == 0:
            for copy in small:
                copy.start()

    barrier = pltpu.get_barrier_semaphore()

    def greet(peer):
        pl.semaphore_signal(barrier, inc=1, device_id=peer, device_id_type=MESH)

    for step in range(1, n):
        greet({"col": lax.rem(col + step, n)})
    pl.when(other)(lambda: greet(column_owner))

    @pl.when(owner)
    def _():
        for step in range(n):
            greet({"chan": upper - 1, "col": lax.rem(col + step, n)})

    row_ids = lax.broadcasted_iota(jnp.int32, weight.shape, 0) + row * wide
    col_ids = lax.broadcasted_iota(jnp.int32, weight.shape, 1) + col * wide
    weight[...] = jnp.where(row_ids == col_ids, 0.0, SHRINK).astype(jnp.bfloat16)

    for copy in small:
        copy.wait()

    group = [slice(h * half, (h + 1) * half) for h in range(HALVES)]
    slot = lax.rem(lax.broadcasted_iota(jnp.int32, (2 * half, wide), 0), half)

    def prepare(k):
        for at in range(0, wide, CHUNK):
            rows = pl.ds(at, CHUNK)
            scale = weight[rows]
            m_re = (mbuf[k, 0, rows] * scale).astype(jnp.float32)
            m_im = (mbuf[k, 1, rows] * scale).astype(jnp.float32)
            v_re = vbuf[k, 0, rows].astype(jnp.float32)
            v_im = vbuf[k, 1, rows].astype(jnp.float32)
            values = (m_re * v_re + m_im * v_im, m_re * v_im - m_im * v_re, m_re * m_re + m_im * m_im)
            for place, value in enumerate(values):
                high = value.astype(jnp.bfloat16)
                low = (value - high.astype(jnp.float32)).astype(jnp.bfloat16)
                into, at_lane = (abuf, 2 * place * wide) if place < 2 else (bbuf, 0)
                into[k, rows, at_lane:at_lane + wide] = high
                into[k, rows, at_lane + wide:at_lane + 2 * wide] = low

    def flip():
        @pl.loop(0, ch)
        def _(k):
            for source, target in ((abuf, aflip), (bbuf, bflip)):
                for at in range(0, source.shape[2], wide):
                    target[k, at:at + wide, :] = source[k, :, at:at + wide].T

    def factors(x_re, x_im):
        by_re = stack_bf16(jnp.concatenate([x_re, x_im], axis=0))
        by_im = stack_bf16(jnp.concatenate([-x_im, x_re], axis=0))
        huge = jnp.maximum(jnp.abs(x_re), jnp.abs(x_im)) > HUGE
        down = jnp.where(huge, HUGE_SHRINK, 1.0)
        square = (x_re * down) * (x_re * down) + (x_im * down) * (x_im * down)
        by_b = stack_bf16(jnp.concatenate([jnp.where(huge, 0.0, square), jnp.where(huge, square, 0.0)], axis=0))
        return jnp.concatenate([by_re, by_re, by_im, by_im], axis=1), jnp.concatenate([by_b, by_b], axis=1)

    def add_channel(totals, by, k, flipped):
        num, den = totals
        a, b, side = (aflip, bflip, 0) if flipped else (abuf, bbuf, 1)
        new_num = dot(by[0], a[k], side)
        new_den = dot(by[1], b[k], side)
        here = slot == k % half
        num = jnp.where(here, new_num[0:2 * half] + new_num[2 * half:4 * half], num)
        den = jnp.where(here, new_den[0:2 * half] + new_den[2 * half:4 * half], den)
        return num, den

    def keep(totals, ref):
        num, den = totals
        ref[0] = num[0:half] * NUM_LOWER
        ref[1] = num[half:2 * half] * NUM_LOWER
        ref[2] = den[0:half] * DEN_LOWER + den[half:2 * half] * HUGE_GROW

    def nothing():
        return (jnp.zeros((2 * half, wide), jnp.float32),) * 2

    def quotient(parts):
        total = [parts[0][place] for place in range(3)]
        for part in parts[1:]:
            for place in range(3):
                total[place] = total[place] + part[place]
        least = jnp.maximum(total[2], LEAST)
        return total[0] / least, total[1] / least

    def wait_bytes(ref, sem):
        pltpu.make_async_copy(ref, ref, sem).wait()

    def deliver(it, h, totals):
        if it == ITERS - 1:
            keep(totals, last.at[h, col])
            for step in farthest_first(n):
                pltpu.make_async_remote_copy(
                    src_ref=last.at[h, col], dst_ref=last.at[h, col],
                    send_sem=last_send.at[h], recv_sem=last_recv.at[h],
                    device_id={"col": lax.rem(col + step, n)}, device_id_type=MESH,
                ).start()
            return

        @pl.when(owner)
        def _():
            keep(totals, sums.at[it, h, 1, col])

        @pl.when(other)
        def _():
            keep(totals, mine.at[it, h])
            pltpu.make_async_remote_copy(
                src_ref=mine.at[it, h], dst_ref=sums.at[it, h, core, col],
                send_sem=sum_send.at[it, h], recv_sem=sum_recv.at[it, h, core],
                device_id=row_owner, device_id_type=MESH,
            ).start()

    def settle(it, h, part):
        wait_bytes(sums.at[it, h, part, 0:n - part], sum_recv.at[it, h, part])
        re, im = quotient([sums.at[it, h, part, peer] for peer in range(n)])
        fresh[it, h, part, 0] = re
        fresh[it, h, part, 1] = im
        if part == 1:
            arrived[it, h, 0] = re
            arrived[it, h, 1] = im
        for step in farthest_first(n) + [0] * (part == 0):
            pltpu.make_async_remote_copy(
                src_ref=fresh.at[it, h, part], dst_ref=arrived.at[it, h],
                send_sem=x_send.at[it, h, part], recv_sem=x_recv.at[it, h],
                device_id={"chan": upper - 1 + part, "row": lax.rem(row + step, n)}, device_id_type=MESH,
            ).start()

    def first_factors(h):
        usable = mcol[group[h], :] > 0
        x = [jnp.where(usable, gcol[group[h], part, :], 0.0) for part in range(2)]
        return factors(*x)

    by = [first_factors(h) for h in range(HALVES)]
    totals = nothing()
    for k in range(ch + 1):
        if k < ch:
            for copy in loads(k):
                copy.wait()
        if k > 0:
            totals = add_channel(totals, by[(k - 1) // half], k - 1, False)
        if k < ch:
            prepare(k)
        if k > 0 and k % half == 0:
            if k == half:
                pl.semaphore_wait(barrier, n - 1 + (core == 0).astype(jnp.int32) + (2 * n - 1) * owner.astype(jnp.int32))
            deliver(0, k // half - 1, totals)
            totals = nothing()

    for it in range(ITERS - 1):
        @pl.when(owner)
        def _():
            for h in range(HALVES):
                for part in (1, 0):
                    settle(it, h, part)

        if it == 0:
            flip()
        for h in range(HALVES):
            pl.when(other)(lambda: wait_bytes(arrived.at[it, h], x_recv.at[it, h]))
            usable = mcol[group[h], :] > 0
            x = []
            for part in range(2):
                value = arrived[it, h, part]
                if it % 2 == 1:
                    value = 0.5 * (value + old[h, part])
                elif it + 1 < ITERS - 1:
                    old[h, part] = value
                x.append(jnp.where(usable, value, 0.0))
            by = factors(*x)
            totals = nothing()
            for k in range(h * half, (h + 1) * half):
                totals = add_channel(totals, by, k, True)
            deliver(it + 1, h, totals)

    copies = []
    for h in range(HALVES):
        wait_bytes(last.at[h, 0:n - 1], last_recv.at[h])
        usable = mrow[group[h], :] > 0
        for part, value in enumerate(quotient([last.at[h, peer] for peer in range(n)])):
            final[group[h], part, :] = jnp.where(usable, value, grow[group[h], part, :])
        copies.append(pltpu.make_async_copy(final.at[group[h]], out.at[group[h]], out_sem.at[h]))
        copies[h].start()

    for it in range(ITERS - 1):
        for h in range(HALVES):
            pl.when(other)(lambda: wait_bytes(mine.at[it, h], sum_send.at[it, h]))

            @pl.when(owner)
            def _():
                for part in range(CORES):
                    wait_bytes(sums.at[0, 0, 0, 0:n - part, 0:2], x_send.at[it, h, part])
    for h in range(HALVES):
        wait_bytes(last.at[h, 0:n - 1], last_send.at[h])
    for copy in copies:
        copy.wait()


def per_device(n, visibility, model, gains_init, antenna_mask):
    assert ITERS == 3
    ch, _, _, rows, wide = visibility.shape
    half = ch // HALVES
    f32, bf16 = jnp.float32, jnp.bfloat16
    hbm = pl.BlockSpec(memory_space=pltpu.HBM)
    dma = pltpu.SemaphoreType.DMA
    gains = pl.pallas_call(
        functools.partial(kernel, n),
        out_shape=jax.ShapeDtypeStruct((ch, 2, wide), f32),
        in_specs=[hbm] * 4,
        out_specs=hbm,
        scratch_shapes=[
            pltpu.VMEM((ch, 2, rows, wide), bf16),
            pltpu.VMEM((ch, 2, rows, wide), bf16),
            pltpu.VMEM((ch, rows, 4 * wide), bf16),
            pltpu.VMEM((ch, rows, 2 * wide), bf16),
            pltpu.VMEM((ch, 4 * wide, rows), bf16),
            pltpu.VMEM((ch, 2 * wide, rows), bf16),
            pltpu.VMEM((rows, wide), bf16),
            pltpu.VMEM((ch, 2, wide), f32),
            pltpu.VMEM((ch, 2, wide), f32),
            pltpu.VMEM((ch, wide), jnp.int32),
            pltpu.VMEM((ch, wide), jnp.int32),
            pltpu.VMEM((HALVES, 2, half, wide), f32),
            pltpu.VMEM((ITERS - 1, HALVES, 3, half, wide), f32),
            pltpu.VMEM((ITERS - 1, HALVES, CORES, n, 3, half, wide), f32),
            pltpu.VMEM((ITERS - 1, HALVES, CORES, 2, half, wide), f32),
            pltpu.VMEM((ITERS - 1, HALVES, 2, half, wide), f32),
            pltpu.VMEM((HALVES, n, 3, half, wide), f32),
            pltpu.VMEM((ch, 2, wide), f32),
            dma((2, ch)),
            dma((4,)),
            dma((ITERS - 1, HALVES)),
            dma((ITERS - 1, HALVES, CORES)),
            dma((ITERS - 1, HALVES, CORES)),
            dma((ITERS - 1, HALVES)),
            dma((HALVES,)),
            dma((HALVES,)),
            dma((HALVES,)),
        ],
        compiler_params=pltpu.CompilerParams(
            collective_id=0, has_side_effects=True, vmem_limit_bytes=60 * 2**20
        ),
        cost_estimate=pl.CostEstimate(flops=2 * 48 * 16 * 256 * 256 * 3, bytes_accessed=4 * 2**20, transcendentals=0),
    )(
        visibility.reshape(ch, 2, rows, wide),
        model.reshape(ch, 2, rows, wide),
        gains_init.reshape(ch, 2, gains_init.shape[3]),
        antenna_mask,
    )
    return gains.reshape(ch, 1, 2, wide)


def solution(mesh):
    n = mesh.shape["col"]
    assert mesh.shape["row"] == n and mesh.shape["chan"] % CORES == 0
    return jax.shard_map(
        functools.partial(per_device, n),
        mesh=mesh,
        in_specs=(
            P("chan", None, None, "row", "col"),
            P("chan", None, None, "row", "col"),
            P("chan", None, None, None),
            P("chan", None),
        ),
        out_specs=P("chan", None, None, "row"),
        check_vma=False,
    )
```

```python
import functools

import jax
import jax.numpy as jnp
from jax import lax
from jax.experimental import pallas as pl
from jax.experimental.pallas import tpu as pltpu
from jax.sharding import PartitionSpec as P

ITERS = 3
HALVES = 2
CORES = 2
MESH = pl.DeviceIdType.MESH
SHRINK = 2.0**-5
HUGE = 2.0**60
HUGE_SHRINK = 2.0**-65
DEN_LOWER = 2.0**-4
HUGE_GROW = 2.0**126
NUM_LOWER = SHRINK * DEN_LOWER
LEAST = SHRINK * NUM_LOWER
CHUNK = 32


def split(x):
    high = x.astype(jnp.bfloat16).astype(jnp.float32)
    return high, x - high


def stack_bf16(x):
    return jnp.concatenate(split(x), axis=0).astype(jnp.bfloat16)


def dot(x, y, side):
    return lax.dot_general(x, y, (((1,), (side,)), ((), ())), preferred_element_type=jnp.float32)


def farthest_first(n):
    return sorted(range(1, n), key=lambda step: -min(step, n - step))


def kernel(
    n, vis, mod, gin, mask, out,
    vbuf, mbuf, abuf, bbuf, aflip, bflip, weight, gcol, grow, mcol, mrow, old,
    mine, sums, fresh, arrived, last, final,
    in_sem, small_sem, sum_send, sum_recv, x_send, x_recv, last_send, last_recv, out_sem,
):
    chan = lax.axis_index("chan")
    row = lax.axis_index("row")
    col = lax.axis_index("col")
    ch, wide = mcol.shape
    half = ch // HALVES
    core = lax.rem(chan, CORES)
    upper = chan - core + 1
    diag = row == col
    owner = jnp.logical_and(diag, core == 1)
    other = jnp.logical_not(owner)
    column_owner = {"chan": upper, "row": col, "col": col}
    row_owner = {"chan": upper, "row": row, "col": row}

    def loads(k):
        return (
            pltpu.make_async_copy(vis.at[k], vbuf.at[k], in_sem.at[0, k]),
            pltpu.make_async_copy(mod.at[k], mbuf.at[k], in_sem.at[1, k]),
        )

    row_at = pl.ds(pl.multiple_of(row * wide, wide), wide)
    col_at = pl.ds(pl.multiple_of(col * wide, wide), wide)
    small = (
        pltpu.make_async_copy(gin.at[:, :, col_at], gcol, small_sem.at[0]),
        pltpu.make_async_copy(mask.at[:, col_at], mcol, small_sem.at[1]),
        pltpu.make_async_copy(mask.at[:, row_at], mrow, small_sem.at[2]),
        pltpu.make_async_copy(gin.at[:, :, row_at], grow, small_sem.at[3]),
    )
    barrier = pltpu.get_barrier_semaphore()

    def greet(peer):
        pl.semaphore_signal(barrier, inc=1, device_id=peer, device_id_type=MESH)

    @pl.when(owner)
    def _():
        for step in farthest_first(n) + [0]:
            for part in range(CORES):
                if part == 0 or step != 0:
                    greet({"chan": upper - 1 + part, "col": lax.rem(col + step, n)})

    for k in range(ch):
        for copy in loads(k):
            copy.start()
        if k == 0:
            for copy in small:
                copy.start()
            pl.when(other)(lambda: greet(column_owner))

    row_ids = lax.broadcasted_iota(jnp.int32, weight.shape, 0) + row * wide
    col_ids = lax.broadcasted_iota(jnp.int32, weight.shape, 1) + col * wide
    weight[...] = jnp.where(row_ids == col_ids, 0.0, SHRINK).astype(jnp.bfloat16)

    for copy in small:
        copy.wait()

    group = [slice(h * half, (h + 1) * half) for h in range(HALVES)]
    slot = lax.rem(lax.broadcasted_iota(jnp.int32, (2 * half, wide), 0), half)

    def prepare(k):
        for at in range(0, wide, CHUNK):
            rows = pl.ds(at, CHUNK)
            scale = weight[rows]
            m_re = (mbuf[k, 0, rows] * scale).astype(jnp.float32)
            m_im = (mbuf[k, 1, rows] * scale).astype(jnp.float32)
            v_re = vbuf[k, 0, rows].astype(jnp.float32)
            v_im = vbuf[k, 1, rows].astype(jnp.float32)
            values = (m_re * v_re + m_im * v_im, m_re * v_im - m_im * v_re, m_re * m_re + m_im * m_im)
            for place, value in enumerate(values):
                high = value.astype(jnp.bfloat16)
                low = (value - high.astype(jnp.float32)).astype(jnp.bfloat16)
                into, at_lane = (abuf, 2 * place * wide) if place < 2 else (bbuf, 0)
                into[k, rows, at_lane:at_lane + wide] = high
                into[k, rows, at_lane + wide:at_lane + 2 * wide] = low

    def flip():
        @pl.loop(0, ch)
        def _(k):
            for source, target in ((abuf, aflip), (bbuf, bflip)):
                for at in range(0, source.shape[2], wide):
                    target[k, at:at + wide, :] = source[k, :, at:at + wide].T

    def factors(x_re, x_im):
        by_re = stack_bf16(jnp.concatenate([x_re, x_im], axis=0))
        by_im = stack_bf16(jnp.concatenate([-x_im, x_re], axis=0))
        huge = jnp.maximum(jnp.abs(x_re), jnp.abs(x_im)) > HUGE
        down = jnp.where(huge, HUGE_SHRINK, 1.0)
        square = (x_re * down) * (x_re * down) + (x_im * down) * (x_im * down)
        by_b = stack_bf16(jnp.concatenate([jnp.where(huge, 0.0, square), jnp.where(huge, square, 0.0)], axis=0))
        return jnp.concatenate([by_re, by_re, by_im, by_im], axis=1), jnp.concatenate([by_b, by_b], axis=1)

    def add_channel(totals, by, k, flipped):
        num, den = totals
        a, b, side = (aflip, bflip, 0) if flipped else (abuf, bbuf, 1)
        new_num = dot(by[0], a[k], side)
        new_den = dot(by[1], b[k], side)
        here = slot == k % half
        num = jnp.where(here, new_num[0:2 * half] + new_num[2 * half:4 * half], num)
        den = jnp.where(here, new_den[0:2 * half] + new_den[2 * half:4 * half], den)
        return num, den

    def keep(totals, ref):
        num, den = totals
        ref[0] = num[0:half] * NUM_LOWER
        ref[1] = num[half:2 * half] * NUM_LOWER
        ref[2] = den[0:half] * DEN_LOWER + den[half:2 * half] * HUGE_GROW

    def nothing():
        return (jnp.zeros((2 * half, wide), jnp.float32),) * 2

    def quotient(parts):
        total = [parts[0][place] for place in range(3)]
        for part in parts[1:]:
            for place in range(3):
                total[place] = total[place] + part[place]
        least = jnp.maximum(total[2], LEAST)
        return total[0] / least, total[1] / least

    def wait_bytes(ref, sem):
        pltpu.make_async_copy(ref, ref, sem).wait()

    def deliver(it, h, totals):
        if it == ITERS - 1:
            keep(totals, last.at[h, col])
            for step in farthest_first(n):
                pltpu.make_async_remote_copy(
                    src_ref=last.at[h, col], dst_ref=last.at[h, col],
                    send_sem=last_send.at[h], recv_sem=last_recv.at[h],
                    device_id={"col": lax.rem(col + step, n)}, device_id_type=MESH,
                ).start()
            return

        @pl.when(owner)
        def _():
            keep(totals, sums.at[it, h, 1, col])

        @pl.when(other)
        def _():
            keep(totals, mine.at[it, h])
            pltpu.make_async_remote_copy(
                src_ref=mine.at[it, h], dst_ref=sums.at[it, h, core, col],
                send_sem=sum_send.at[it, h], recv_sem=sum_recv.at[it, h, core],
                device_id=row_owner, device_id_type=MESH,
            ).start()

    def settle(it, h, part):
        wait_bytes(sums.at[it, h, part, 0:n - part], sum_recv.at[it, h, part])
        re, im = quotient([sums.at[it, h, part, peer] for peer in range(n)])
        fresh[it, h, part, 0] = re
        fresh[it, h, part, 1] = im
        if part == 1:
            arrived[it, h, 0] = re
            arrived[it, h, 1] = im
        for step in farthest_first(n) + [0] * (part == 0):
            pltpu.make_async_remote_copy(
                src_ref=fresh.at[it, h, part], dst_ref=arrived.at[it, h],
                send_sem=x_send.at[it, h, part], recv_sem=x_recv.at[it, h],
                device_id={"chan": upper - 1 + part, "row": lax.rem(row + step, n)}, device_id_type=MESH,
            ).start()

    def first_factors(h):
        usable = mcol[group[h], :] > 0
        x = [jnp.where(usable, gcol[group[h], part, :], 0.0) for part in range(2)]
        return factors(*x)

    by = [first_factors(h) for h in range(HALVES)]
    totals = nothing()
    for k in range(ch + 1):
        if k < ch:
            for copy in loads(k):
                copy.wait()
        if k > 0:
            totals = add_channel(totals, by[(k - 1) // half], k - 1, False)
        if k < ch:
            prepare(k)
        if k > 0 and k % half == 0:
            if k == half:
                pl.when(other)(lambda: pl.semaphore_wait(barrier, 1))
            deliver(0, k // half - 1, totals)
            totals = nothing()

    for it in range(ITERS - 1):
        @pl.when(owner)
        def _():
            if it == 0:
                pl.semaphore_wait(barrier, CORES * n - 1)
            for h in range(HALVES):
                for part in (1, 0):
                    settle(it, h, part)

        if it == 0:
            flip()
        for h in range(HALVES):
            pl.when(other)(lambda: wait_bytes(arrived.at[it, h], x_recv.at[it, h]))
            usable = mcol[group[h], :] > 0
            x = []
            for part in range(2):
                value = arrived[it, h, part]
                if it % 2 == 1:
                    value = 0.5 * (value + old[h, part])
                elif it + 1 < ITERS - 1:
                    old[h, part] = value
                x.append(jnp.where(usable, value, 0.0))
            by = factors(*x)
            totals = nothing()
            for k in range(h * half, (h + 1) * half):
                totals = add_channel(totals, by, k, True)
            deliver(it + 1, h, totals)

    copies = []
    for h in range(HALVES):
        wait_bytes(last.at[h, 0:n - 1], last_recv.at[h])
        usable = mrow[group[h], :] > 0
        for part, value in enumerate(quotient([last.at[h, peer] for peer in range(n)])):
            final[group[h], part, :] = jnp.where(usable, value, grow[group[h], part, :])
        copies.append(pltpu.make_async_copy(final.at[group[h]], out.at[group[h]], out_sem.at[h]))
        copies[h].start()

    for it in range(ITERS - 1):
        for h in range(HALVES):
            pl.when(other)(lambda: wait_bytes(mine.at[it, h], sum_send.at[it, h]))

            @pl.when(owner)
            def _():
                for part in range(CORES):
                    wait_bytes(sums.at[0, 0, 0, 0:n - part, 0:2], x_send.at[it, h, part])
    for h in range(HALVES):
        wait_bytes(last.at[h, 0:n - 1], last_send.at[h])
    for copy in copies:
        copy.wait()


def per_device(n, visibility, model, gains_init, antenna_mask):
    assert ITERS == 3
    ch, _, _, rows, wide = visibility.shape
    half = ch // HALVES
    f32, bf16 = jnp.float32, jnp.bfloat16
    hbm = pl.BlockSpec(memory_space=pltpu.HBM)
    dma = pltpu.SemaphoreType.DMA
    gains = pl.pallas_call(
        functools.partial(kernel, n),
        out_shape=jax.ShapeDtypeStruct((ch, 2, wide), f32),
        in_specs=[hbm] * 4,
        out_specs=hbm,
        scratch_shapes=[
            pltpu.VMEM((ch, 2, rows, wide), bf16),
            pltpu.VMEM((ch, 2, rows, wide), bf16),
            pltpu.VMEM((ch, rows, 4 * wide), bf16),
            pltpu.VMEM((ch, rows, 2 * wide), bf16),
            pltpu.VMEM((ch, 4 * wide, rows), bf16),
            pltpu.VMEM((ch, 2 * wide, rows), bf16),
            pltpu.VMEM((rows, wide), bf16),
            pltpu.VMEM((ch, 2, wide), f32),
            pltpu.VMEM((ch, 2, wide), f32),
            pltpu.VMEM((ch, wide), jnp.int32),
            pltpu.VMEM((ch, wide), jnp.int32),
            pltpu.VMEM((HALVES, 2, half, wide), f32),
            pltpu.VMEM((ITERS - 1, HALVES, 3, half, wide), f32),
            pltpu.VMEM((ITERS - 1, HALVES, CORES, n, 3, half, wide), f32),
            pltpu.VMEM((ITERS - 1, HALVES, CORES, 2, half, wide), f32),
            pltpu.VMEM((ITERS - 1, HALVES, 2, half, wide), f32),
            pltpu.VMEM((HALVES, n, 3, half, wide), f32),
            pltpu.VMEM((ch, 2, wide), f32),
            dma((2, ch)),
            dma((4,)),
            dma((ITERS - 1, HALVES)),
            dma((ITERS - 1, HALVES, CORES)),
            dma((ITERS - 1, HALVES, CORES)),
            dma((ITERS - 1, HALVES)),
            dma((HALVES,)),
            dma((HALVES,)),
            dma((HALVES,)),
        ],
        compiler_params=pltpu.CompilerParams(
            collective_id=0, has_side_effects=True, vmem_limit_bytes=55184 * 2**10
        ),
        cost_estimate=pl.CostEstimate(flops=2 * 48 * 16 * 256 * 256 * 3, bytes_accessed=4 * 2**20, transcendentals=0),
    )(
        visibility.reshape(ch, 2, rows, wide),
        model.reshape(ch, 2, rows, wide),
        gains_init.reshape(ch, 2, gains_init.shape[3]),
        antenna_mask,
    )
    return gains.reshape(ch, 1, 2, wide)


def solution(mesh):
    n = mesh.shape["col"]
    assert mesh.shape["row"] == n and mesh.shape["chan"] % CORES == 0
    return jax.shard_map(
        functools.partial(per_device, n),
        mesh=mesh,
        in_specs=(
            P("chan", None, None, "row", "col"),
            P("chan", None, None, "row", "col"),
            P("chan", None, None, None),
            P("chan", None),
        ),
        out_specs=P("chan", None, None, "row"),
        check_vma=False,
    )
```

```python
import functools

import jax
import jax.numpy as jnp
from jax import lax
from jax.experimental import pallas as pl
from jax.experimental.pallas import tpu as pltpu
from jax.sharding import PartitionSpec as P

ITERS = 3
HALVES = 2
CORES = 2
MESH = pl.DeviceIdType.MESH
SHRINK = 2.0**-5
HUGE = 2.0**60
HUGE_SHRINK = 2.0**-65
DEN_LOWER = 2.0**-4
HUGE_GROW = 2.0**126
NUM_LOWER = SHRINK * DEN_LOWER
LEAST = SHRINK * NUM_LOWER
CHUNK = 32
FIRST = 3


def split(x):
    high = x.astype(jnp.bfloat16).astype(jnp.float32)
    return high, x - high


def stack_bf16(x):
    return jnp.concatenate(split(x), axis=0).astype(jnp.bfloat16)


def dot(x, y, side):
    return lax.dot_general(x, y, (((1,), (side,)), ((), ())), preferred_element_type=jnp.float32)


def farthest_first(n):
    return sorted(range(1, n), key=lambda step: -min(step, n - step))


def kernel(
    n, vis, mod, gin, mask, out,
    vbuf, mbuf, abuf, bbuf, aflip, bflip, weight, gcol, grow, mcol, mrow, old,
    mine, sums, fresh, arrived, last,
    in_sem, small_sem, sum_send, sum_recv, x_send, x_recv, last_send, last_recv,
):
    chan = lax.axis_index("chan")
    row = lax.axis_index("row")
    col = lax.axis_index("col")
    ch, wide = mcol.shape
    half = ch // HALVES
    core = lax.rem(chan, CORES)
    upper = chan - core + 1
    diag = row == col
    owner = jnp.logical_and(diag, core == 1)
    other = jnp.logical_not(owner)
    column_owner = {"chan": upper, "row": col, "col": col}
    row_owner = {"chan": upper, "row": row, "col": row}

    def loads(k):
        return (
            pltpu.make_async_copy(vis.at[k], vbuf.at[k], in_sem.at[0, k]),
            pltpu.make_async_copy(mod.at[k], mbuf.at[k], in_sem.at[1, k]),
        )

    row_at = pl.ds(pl.multiple_of(row * wide, wide), wide)
    col_at = pl.ds(pl.multiple_of(col * wide, wide), wide)
    small = (
        pltpu.make_async_copy(gin.at[:, :, col_at], gcol, small_sem.at[0]),
        pltpu.make_async_copy(mask.at[:, col_at], mcol, small_sem.at[1]),
        pltpu.make_async_copy(mask.at[:, row_at], mrow, small_sem.at[2]),
        pltpu.make_async_copy(gin.at[:, :, row_at], grow, small_sem.at[3]),
    )
    barrier = pltpu.get_barrier_semaphore()

    def greet(peer):
        pl.semaphore_signal(barrier, inc=1, device_id=peer, device_id_type=MESH)

    @pl.when(owner)
    def _():
        for step in farthest_first(n) + [0]:
            for part in range(CORES):
                if part == 0 or step != 0:
                    greet({"chan": upper - 1 + part, "col": lax.rem(col + step, n)})

    for k in range(ch):
        for copy in loads(k):
            copy.start(priority=int(k >= FIRST))
        if k == 0:
            for copy in small:
                copy.start()
            pl.when(other)(lambda: greet(column_owner))

    row_ids = lax.broadcasted_iota(jnp.int32, weight.shape, 0) + row * wide
    col_ids = lax.broadcasted_iota(jnp.int32, weight.shape, 1) + col * wide
    weight[...] = jnp.where(row_ids == col_ids, 0.0, SHRINK).astype(jnp.bfloat16)

    group = [slice(h * half, (h + 1) * half) for h in range(HALVES)]
    slot = lax.rem(lax.broadcasted_iota(jnp.int32, (2 * half, wide), 0), half)

    def prepare(k):
        for at in range(0, wide, CHUNK):
            rows = pl.ds(at, CHUNK)
            scale = weight[rows]
            m_re = (mbuf[k, 0, rows] * scale).astype(jnp.float32)
            m_im = (mbuf[k, 1, rows] * scale).astype(jnp.float32)
            v_re = vbuf[k, 0, rows].astype(jnp.float32)
            v_im = vbuf[k, 1, rows].astype(jnp.float32)
            values = (m_re * v_re + m_im * v_im, m_re * v_im - m_im * v_re, m_re * m_re + m_im * m_im)
            for place, value in enumerate(values):
                high = value.astype(jnp.bfloat16)
                low = (value - high.astype(jnp.float32)).astype(jnp.bfloat16)
                into, at_lane = (abuf, 2 * place * wide) if place < 2 else (bbuf, 0)
                into[k, rows, at_lane:at_lane + wide] = high
                into[k, rows, at_lane + wide:at_lane + 2 * wide] = low

    def flip():
        @pl.loop(0, ch)
        def _(k):
            for source, target in ((abuf, aflip), (bbuf, bflip)):
                for at in range(0, source.shape[2], wide):
                    target[k, at:at + wide, :] = source[k, :, at:at + wide].T

    def factors(x_re, x_im):
        by_re = stack_bf16(jnp.concatenate([x_re, x_im], axis=0))
        by_im = stack_bf16(jnp.concatenate([-x_im, x_re], axis=0))
        huge = jnp.maximum(jnp.abs(x_re), jnp.abs(x_im)) > HUGE
        down = jnp.where(huge, HUGE_SHRINK, 1.0)
        square = (x_re * down) * (x_re * down) + (x_im * down) * (x_im * down)
        by_b = stack_bf16(jnp.concatenate([jnp.where(huge, 0.0, square), jnp.where(huge, square, 0.0)], axis=0))
        return jnp.concatenate([by_re, by_re, by_im, by_im], axis=1), jnp.concatenate([by_b, by_b], axis=1)

    def add_channel(totals, by, k, flipped):
        num, den = totals
        a, b, side = (aflip, bflip, 0) if flipped else (abuf, bbuf, 1)
        new_num = dot(by[0], a[k], side)
        new_den = dot(by[1], b[k], side)
        here = slot == k % half
        num = jnp.where(here, new_num[0:2 * half] + new_num[2 * half:4 * half], num)
        den = jnp.where(here, new_den[0:2 * half] + new_den[2 * half:4 * half], den)
        return num, den

    def keep(totals, ref):
        num, den = totals
        ref[0] = num[0:half] * NUM_LOWER
        ref[1] = num[half:2 * half] * NUM_LOWER
        ref[2] = den[0:half] * DEN_LOWER + den[half:2 * half] * HUGE_GROW

    def nothing():
        return (jnp.zeros((2 * half, wide), jnp.float32),) * 2

    def quotient(parts):
        total = [parts[0][place] for place in range(3)]
        for part in parts[1:]:
            for place in range(3):
                total[place] = total[place] + part[place]
        least = jnp.maximum(total[2], LEAST)
        return total[0] / least, total[1] / least

    def wait_bytes(ref, sem):
        pltpu.make_async_copy(ref, ref, sem).wait()

    def deliver(it, h, totals):
        if it == ITERS - 1:
            keep(totals, last.at[h, col])
            for step in farthest_first(n):
                pltpu.make_async_remote_copy(
                    src_ref=last.at[h, col], dst_ref=last.at[h, col],
                    send_sem=last_send.at[h], recv_sem=last_recv.at[h],
                    device_id={"col": lax.rem(col + step, n)}, device_id_type=MESH,
                ).start()
            return

        @pl.when(owner)
        def _():
            keep(totals, sums.at[it, h, 1, col])

        @pl.when(other)
        def _():
            keep(totals, mine.at[it, h])
            pltpu.make_async_remote_copy(
                src_ref=mine.at[it, h], dst_ref=sums.at[it, h, core, col],
                send_sem=sum_send.at[it, h], recv_sem=sum_recv.at[it, h, core],
                device_id=row_owner, device_id_type=MESH,
            ).start()

    def settle(it, h, part):
        wait_bytes(sums.at[it, h, part, 0:n - part], sum_recv.at[it, h, part])
        re, im = quotient([sums.at[it, h, part, peer] for peer in range(n)])
        fresh[it, h, part, 0] = re
        fresh[it, h, part, 1] = im
        if part == 1:
            arrived[it, h, 0] = re
            arrived[it, h, 1] = im
        for step in farthest_first(n) + [0] * (part == 0):
            pltpu.make_async_remote_copy(
                src_ref=fresh.at[it, h, part], dst_ref=arrived.at[it, h],
                send_sem=x_send.at[it, h, part], recv_sem=x_recv.at[it, h],
                device_id={"chan": upper - 1 + part, "row": lax.rem(row + step, n)}, device_id_type=MESH,
            ).start()

    def first_factors(h):
        usable = mcol[group[h], :] > 0
        x = [jnp.where(usable, gcol[group[h], part, :], 0.0) for part in range(2)]
        return factors(*x)

    totals = nothing()
    ready = 0
    for k in range(ch + 1):
        if k == ready < ch:
            until = FIRST if k == 0 else ch
            for arrival in range(k, until):
                for copy in loads(arrival):
                    copy.wait()
            ready = until
        if k == 1:
            for copy in small:
                copy.wait()
            by = [first_factors(h) for h in range(HALVES)]
        if k > 0:
            totals = add_channel(totals, by[(k - 1) // half], k - 1, False)
        if k < ch:
            prepare(k)
        if k > 0 and k % half == 0:
            if k == half:
                pl.when(other)(lambda: pl.semaphore_wait(barrier, 1))
            deliver(0, k // half - 1, totals)
            totals = nothing()

    for it in range(ITERS - 1):
        @pl.when(owner)
        def _():
            if it == 0:
                pl.semaphore_wait(barrier, CORES * n - 1)
            for h in range(HALVES):
                for part in (1, 0):
                    settle(it, h, part)

        if it == 0:
            flip()
        for h in range(HALVES):
            pl.when(other)(lambda: wait_bytes(arrived.at[it, h], x_recv.at[it, h]))
            usable = mcol[group[h], :] > 0
            x = []
            for part in range(2):
                value = arrived[it, h, part]
                if it % 2 == 1:
                    value = 0.5 * (value + old[h, part])
                elif it + 1 < ITERS - 1:
                    old[h, part] = value
                x.append(jnp.where(usable, value, 0.0))
            by = factors(*x)
            totals = nothing()
            for k in range(h * half, (h + 1) * half):
                totals = add_channel(totals, by, k, True)
            deliver(it + 1, h, totals)

    for h in range(HALVES):
        wait_bytes(last.at[h, 0:n - 1], last_recv.at[h])
        usable = mrow[group[h], :] > 0
        for part, value in enumerate(quotient([last.at[h, peer] for peer in range(n)])):
            out[group[h], part, :] = jnp.where(usable, value, grow[group[h], part, :])

    for it in range(ITERS - 1):
        for h in range(HALVES):
            pl.when(other)(lambda: wait_bytes(mine.at[it, h], sum_send.at[it, h]))

            @pl.when(owner)
            def _():
                for part in range(CORES):
                    wait_bytes(sums.at[0, 0, 0, 0:n - part, 0:2], x_send.at[it, h, part])
    for h in range(HALVES):
        wait_bytes(last.at[h, 0:n - 1], last_send.at[h])


def per_device(n, visibility, model, gains_init, antenna_mask):
    assert ITERS == 3
    ch, _, _, rows, wide = visibility.shape
    half = ch // HALVES
    f32, bf16 = jnp.float32, jnp.bfloat16
    hbm = pl.BlockSpec(memory_space=pltpu.HBM)
    dma = pltpu.SemaphoreType.DMA
    gains = pl.pallas_call(
        functools.partial(kernel, n),
        out_shape=jax.ShapeDtypeStruct((ch, 2, wide), f32),
        in_specs=[hbm] * 4,
        out_specs=pl.BlockSpec(memory_space=pltpu.VMEM),
        scratch_shapes=[
            pltpu.VMEM((ch, 2, rows, wide), bf16),
            pltpu.VMEM((ch, 2, rows, wide), bf16),
            pltpu.VMEM((ch, rows, 4 * wide), bf16),
            pltpu.VMEM((ch, rows, 2 * wide), bf16),
            pltpu.VMEM((ch, 4 * wide, rows), bf16),
            pltpu.VMEM((ch, 2 * wide, rows), bf16),
            pltpu.VMEM((rows, wide), bf16),
            pltpu.VMEM((ch, 2, wide), f32),
            pltpu.VMEM((ch, 2, wide), f32),
            pltpu.VMEM((ch, wide), jnp.int32),
            pltpu.VMEM((ch, wide), jnp.int32),
            pltpu.VMEM((HALVES, 2, half, wide), f32),
            pltpu.VMEM((ITERS - 1, HALVES, 3, half, wide), f32),
            pltpu.VMEM((ITERS - 1, HALVES, CORES, n, 3, half, wide), f32),
            pltpu.VMEM((ITERS - 1, HALVES, CORES, 2, half, wide), f32),
            pltpu.VMEM((ITERS - 1, HALVES, 2, half, wide), f32),
            pltpu.VMEM((HALVES, n, 3, half, wide), f32),
            dma((2, ch)),
            dma((4,)),
            dma((ITERS - 1, HALVES)),
            dma((ITERS - 1, HALVES, CORES)),
            dma((ITERS - 1, HALVES, CORES)),
            dma((ITERS - 1, HALVES)),
            dma((HALVES,)),
            dma((HALVES,)),
        ],
        compiler_params=pltpu.CompilerParams(
            collective_id=0, has_side_effects=True, vmem_limit_bytes=55184 * 2**10
        ),
        cost_estimate=pl.CostEstimate(flops=2 * 48 * 16 * 256 * 256 * 3, bytes_accessed=4 * 2**20, transcendentals=0),
    )(
        visibility.reshape(ch, 2, rows, wide),
        model.reshape(ch, 2, rows, wide),
        gains_init.reshape(ch, 2, gains_init.shape[3]),
        antenna_mask,
    )
    return gains.reshape(ch, 1, 2, wide)


def solution(mesh):
    n = mesh.shape["col"]
    assert mesh.shape["row"] == n and mesh.shape["chan"] % CORES == 0
    return jax.shard_map(
        functools.partial(per_device, n),
        mesh=mesh,
        in_specs=(
            P("chan", None, None, "row", "col"),
            P("chan", None, None, "row", "col"),
            P("chan", None, None, None),
            P("chan", None),
        ),
        out_specs=P("chan", None, None, "row"),
        check_vma=False,
    )
```

```python
import functools

import jax
import jax.numpy as jnp
from jax import lax
from jax.experimental import pallas as pl
from jax.experimental.pallas import tpu as pltpu
from jax.sharding import PartitionSpec as P

ITERS = 3
HALVES = 2
CORES = 2
DIRECT = ITERS - 2
MESH = pl.DeviceIdType.MESH
SHRINK = 2.0**-5
HUGE = 2.0**60
HUGE_SHRINK = 2.0**-65
DEN_LOWER = 2.0**-4
HUGE_GROW = 2.0**126
NUM_LOWER = SHRINK * DEN_LOWER
LEAST = SHRINK * NUM_LOWER
CHUNK = 32
FIRST = 3


def split(x):
    high = x.astype(jnp.bfloat16).astype(jnp.float32)
    return high, x - high


def stack_bf16(x):
    return jnp.concatenate(split(x), axis=0).astype(jnp.bfloat16)


def dot(x, y, side):
    return lax.dot_general(x, y, (((1,), (side,)), ((), ())), preferred_element_type=jnp.float32)


def farthest_first(n):
    return sorted(range(1, n), key=lambda step: -min(step, n - step))


def nearest_to_zero(n):
    return sorted(range(n), key=lambda place: min(place, n - place))


def kernel(
    n, vis, mod, gin, mask, out,
    vbuf, mbuf, abuf, bbuf, aflip, bflip, weight, gcol, grow, mcol, mrow, old,
    mine, sums, fresh, arrived, last, direct,
    in_sem, small_sem, sum_send, sum_recv, x_send, x_recv, last_send, last_recv, direct_send, direct_recv,
):
    chan = lax.axis_index("chan")
    row = lax.axis_index("row")
    col = lax.axis_index("col")
    ch, wide = mcol.shape
    half = ch // HALVES
    core = lax.rem(chan, CORES)
    upper = chan - core + 1
    diag = row == col
    owner = jnp.logical_and(diag, core == 1)
    other = jnp.logical_not(owner)
    alone = jnp.logical_and(row == 0, col == 0)
    distant = 1 - alone.astype(jnp.int32)
    column_owner = {"chan": upper, "row": col, "col": col}
    row_owner = {"chan": upper, "row": row, "col": row}

    def loads(k):
        return (
            pltpu.make_async_copy(vis.at[k], vbuf.at[k], in_sem.at[0, k]),
            pltpu.make_async_copy(mod.at[k], mbuf.at[k], in_sem.at[1, k]),
        )

    row_at = pl.ds(pl.multiple_of(row * wide, wide), wide)
    col_at = pl.ds(pl.multiple_of(col * wide, wide), wide)
    small = (
        pltpu.make_async_copy(gin.at[:, :, col_at], gcol, small_sem.at[0]),
        pltpu.make_async_copy(mask.at[:, col_at], mcol, small_sem.at[1]),
        pltpu.make_async_copy(mask.at[:, row_at], mrow, small_sem.at[2]),
        pltpu.make_async_copy(gin.at[:, :, row_at], grow, small_sem.at[3]),
    )
    barrier = pltpu.get_barrier_semaphore()

    def greet(peer):
        pl.semaphore_signal(barrier, inc=1, device_id=peer, device_id_type=MESH)

    @pl.when(owner)
    def _():
        for step in farthest_first(n) + [0]:
            for part in range(CORES):
                if part == 0 or step != 0:
                    greet({"chan": upper - 1 + part, "col": lax.rem(col + step, n)})

    @pl.when(row == 0)
    def _():
        for peer in range(n):
            pl.when(jnp.logical_or(col != 0, peer != 0))(lambda: greet({"row": col, "col": peer}))

    for k in range(ch):
        for copy in loads(k):
            copy.start(priority=int(k >= FIRST))
        if k == 0:
            for copy in small:
                copy.start()
            pl.when(other)(lambda: greet(column_owner))

    row_ids = lax.broadcasted_iota(jnp.int32, weight.shape, 0) + row * wide
    col_ids = lax.broadcasted_iota(jnp.int32, weight.shape, 1) + col * wide
    weight[...] = jnp.where(row_ids == col_ids, 0.0, SHRINK).astype(jnp.bfloat16)

    group = [slice(h * half, (h + 1) * half) for h in range(HALVES)]
    slot = lax.rem(lax.broadcasted_iota(jnp.int32, (2 * half, wide), 0), half)

    def prepare(k):
        for at in range(0, wide, CHUNK):
            rows = pl.ds(at, CHUNK)
            scale = weight[rows]
            m_re = (mbuf[k, 0, rows] * scale).astype(jnp.float32)
            m_im = (mbuf[k, 1, rows] * scale).astype(jnp.float32)
            v_re = vbuf[k, 0, rows].astype(jnp.float32)
            v_im = vbuf[k, 1, rows].astype(jnp.float32)
            values = (m_re * v_re + m_im * v_im, m_re * v_im - m_im * v_re, m_re * m_re + m_im * m_im)
            for place, value in enumerate(values):
                high = value.astype(jnp.bfloat16)
                low = (value - high.astype(jnp.float32)).astype(jnp.bfloat16)
                into, at_lane = (abuf, 2 * place * wide) if place < 2 else (bbuf, 0)
                into[k, rows, at_lane:at_lane + wide] = high
                into[k, rows, at_lane + wide:at_lane + 2 * wide] = low

    def flip():
        @pl.loop(0, ch)
        def _(k):
            for source, target in ((abuf, aflip), (bbuf, bflip)):
                for at in range(0, source.shape[2], wide):
                    target[k, at:at + wide, :] = source[k, :, at:at + wide].T

    def factors(x_re, x_im):
        by_re = stack_bf16(jnp.concatenate([x_re, x_im], axis=0))
        by_im = stack_bf16(jnp.concatenate([-x_im, x_re], axis=0))
        huge = jnp.maximum(jnp.abs(x_re), jnp.abs(x_im)) > HUGE
        down = jnp.where(huge, HUGE_SHRINK, 1.0)
        square = (x_re * down) * (x_re * down) + (x_im * down) * (x_im * down)
        by_b = stack_bf16(jnp.concatenate([jnp.where(huge, 0.0, square), jnp.where(huge, square, 0.0)], axis=0))
        return jnp.concatenate([by_re, by_re, by_im, by_im], axis=1), jnp.concatenate([by_b, by_b], axis=1)

    def add_channel(totals, by, k, flipped):
        num, den = totals
        a, b, side = (aflip, bflip, 0) if flipped else (abuf, bbuf, 1)
        new_num = dot(by[0], a[k], side)
        new_den = dot(by[1], b[k], side)
        here = slot == k % half
        num = jnp.where(here, new_num[0:2 * half] + new_num[2 * half:4 * half], num)
        den = jnp.where(here, new_den[0:2 * half] + new_den[2 * half:4 * half], den)
        return num, den

    def keep(totals, ref):
        num, den = totals
        ref[0] = num[0:half] * NUM_LOWER
        ref[1] = num[half:2 * half] * NUM_LOWER
        ref[2] = den[0:half] * DEN_LOWER + den[half:2 * half] * HUGE_GROW

    def nothing():
        return (jnp.zeros((2 * half, wide), jnp.float32),) * 2

    def quotient(parts):
        total = [parts[0][place] for place in range(3)]
        for part in parts[1:]:
            for place in range(3):
                total[place] = total[place] + part[place]
        least = jnp.maximum(total[2], LEAST)
        return total[0] / least, total[1] / least

    def wait_bytes(ref, sem):
        pltpu.make_async_copy(ref, ref, sem).wait()

    def deliver(it, h, totals):
        if it == ITERS - 1:
            keep(totals, last.at[h, col])
            for peer in nearest_to_zero(n):
                pl.when(col != peer)(pltpu.make_async_remote_copy(
                    src_ref=last.at[h, col], dst_ref=last.at[h, col],
                    send_sem=last_send.at[h], recv_sem=last_recv.at[h],
                    device_id={"col": peer}, device_id_type=MESH,
                ).start)
            return

        @pl.when(owner)
        def _():
            keep(totals, sums.at[it, h, 1, col])

        @pl.when(other)
        def _():
            keep(totals, mine.at[it, h])
            pltpu.make_async_remote_copy(
                src_ref=mine.at[it, h], dst_ref=sums.at[it, h, core, col],
                send_sem=sum_send.at[it, h], recv_sem=sum_recv.at[it, h, core],
                device_id=row_owner, device_id_type=MESH,
            ).start()

        if it == DIRECT:
            pl.when(owner)(lambda: keep(totals, mine.at[it, h]))
            pl.when(alone)(lambda: keep(totals, direct.at[h, col]))
            pl.when(jnp.logical_not(alone))(pltpu.make_async_remote_copy(
                src_ref=mine.at[it, h], dst_ref=direct.at[h, col],
                send_sem=direct_send.at[h], recv_sem=direct_recv.at[h],
                device_id={"row": 0, "col": row}, device_id_type=MESH,
            ).start)

    def settle(it, h, part):
        wait_bytes(sums.at[it, h, part, 0:n - part], sum_recv.at[it, h, part])
        re, im = quotient([sums.at[it, h, part, peer] for peer in range(n)])
        fresh[it, h, part, 0] = re
        fresh[it, h, part, 1] = im
        if part == 1:
            arrived[it, h, 0] = re
            arrived[it, h, 1] = im
        def send_to(peer):
            pltpu.make_async_remote_copy(
                src_ref=fresh.at[it, h, part], dst_ref=arrived.at[it, h],
                send_sem=x_send.at[it, h, part], recv_sem=x_recv.at[it, h],
                device_id={"chan": upper - 1 + part, "row": peer}, device_id_type=MESH,
            ).start()

        if it == DIRECT:
            for peer in range(1, n):
                if part == 0:
                    send_to(peer)
                else:
                    pl.when(row != peer)(lambda: send_to(peer))
        else:
            for step in farthest_first(n) + [0] * (part == 0):
                send_to(lax.rem(row + step, n))

    def first_factors(h):
        usable = mcol[group[h], :] > 0
        x = [jnp.where(usable, gcol[group[h], part, :], 0.0) for part in range(2)]
        return factors(*x)

    totals = nothing()
    ready = 0
    for k in range(ch + 1):
        if k == ready < ch:
            until = FIRST if k == 0 else ch
            for arrival in range(k, until):
                for copy in loads(arrival):
                    copy.wait()
            ready = until
        if k == 1:
            for copy in small:
                copy.wait()
            by = [first_factors(h) for h in range(HALVES)]
        if k > 0:
            totals = add_channel(totals, by[(k - 1) // half], k - 1, False)
        if k < ch:
            prepare(k)
        if k > 0 and k % half == 0:
            if k == half:
                pl.when(other)(lambda: pl.semaphore_wait(barrier, 1 + distant))
            deliver(0, k // half - 1, totals)
            totals = nothing()

    for it in range(ITERS - 1):
        @pl.when(owner)
        def _():
            if it == 0:
                pl.semaphore_wait(barrier, CORES * n - 1 + distant)
            for h in range(HALVES):
                for part in (1, 0):
                    settle(it, h, part)

        if it == 0:
            flip()
        for h in range(HALVES):
            if it == DIRECT:
                @pl.when(row == 0)
                def _():
                    pl.when(col == 0)(lambda: wait_bytes(direct.at[h, 0:n - 1], direct_recv.at[h]))
                    pl.when(col != 0)(lambda: wait_bytes(direct.at[h], direct_recv.at[h]))
                    for part, value in enumerate(quotient([direct.at[h, peer] for peer in range(n)])):
                        arrived[it, h, part] = value

                pl.when(jnp.logical_and(other, row != 0))(lambda: wait_bytes(arrived.at[it, h], x_recv.at[it, h]))
            else:
                pl.when(other)(lambda: wait_bytes(arrived.at[it, h], x_recv.at[it, h]))
            usable = mcol[group[h], :] > 0
            x = []
            for part in range(2):
                value = arrived[it, h, part]
                if it % 2 == 1:
                    value = 0.5 * (value + old[h, part])
                elif it + 1 < ITERS - 1:
                    old[h, part] = value
                x.append(jnp.where(usable, value, 0.0))
            by = factors(*x)
            totals = nothing()
            for k in range(h * half, (h + 1) * half):
                totals = add_channel(totals, by, k, True)
            deliver(it + 1, h, totals)

    for h in range(HALVES):
        wait_bytes(last.at[h, 0:n - 1], last_recv.at[h])
        usable = mrow[group[h], :] > 0
        for part, value in enumerate(quotient([last.at[h, peer] for peer in range(n)])):
            out[group[h], part, :] = jnp.where(usable, value, grow[group[h], part, :])

    for it in range(ITERS - 1):
        for h in range(HALVES):
            pl.when(other)(lambda: wait_bytes(mine.at[it, h], sum_send.at[it, h]))

            @pl.when(owner)
            def _():
                if it == DIRECT:
                    wait_bytes(sums.at[0, 0, 0, 0:n - 1, 0:2], x_send.at[it, h, 0])
                    pl.when(row == 0)(lambda: wait_bytes(sums.at[0, 0, 0, 0:n - 1, 0:2], x_send.at[it, h, 1]))
                    if n > 2:
                        pl.when(row != 0)(lambda: wait_bytes(sums.at[0, 0, 0, 0:n - 2, 0:2], x_send.at[it, h, 1]))
                else:
                    for part in range(CORES):
                        wait_bytes(sums.at[0, 0, 0, 0:n - part, 0:2], x_send.at[it, h, part])
    for h in range(HALVES):
        pl.when(jnp.logical_or(row != 0, col != 0))(lambda: wait_bytes(mine.at[0, h], direct_send.at[h]))
        wait_bytes(last.at[h, 0:n - 1], last_send.at[h])


def per_device(n, visibility, model, gains_init, antenna_mask):
    assert ITERS == 3
    ch, _, _, rows, wide = visibility.shape
    half = ch // HALVES
    f32, bf16 = jnp.float32, jnp.bfloat16
    hbm = pl.BlockSpec(memory_space=pltpu.HBM)
    dma = pltpu.SemaphoreType.DMA
    gains = pl.pallas_call(
        functools.partial(kernel, n),
        out_shape=jax.ShapeDtypeStruct((ch, 2, wide), f32),
        in_specs=[hbm] * 4,
        out_specs=pl.BlockSpec(memory_space=pltpu.VMEM),
        scratch_shapes=[
            pltpu.VMEM((ch, 2, rows, wide), bf16),
            pltpu.VMEM((ch, 2, rows, wide), bf16),
            pltpu.VMEM((ch, rows, 4 * wide), bf16),
            pltpu.VMEM((ch, rows, 2 * wide), bf16),
            pltpu.VMEM((ch, 4 * wide, rows), bf16),
            pltpu.VMEM((ch, 2 * wide, rows), bf16),
            pltpu.VMEM((rows, wide), bf16),
            pltpu.VMEM((ch, 2, wide), f32),
            pltpu.VMEM((ch, 2, wide), f32),
            pltpu.VMEM((ch, wide), jnp.int32),
            pltpu.VMEM((ch, wide), jnp.int32),
            pltpu.VMEM((HALVES, 2, half, wide), f32),
            pltpu.VMEM((ITERS - 1, HALVES, 3, half, wide), f32),
            pltpu.VMEM((ITERS - 1, HALVES, CORES, n, 3, half, wide), f32),
            pltpu.VMEM((ITERS - 1, HALVES, CORES, 2, half, wide), f32),
            pltpu.VMEM((ITERS - 1, HALVES, 2, half, wide), f32),
            pltpu.VMEM((HALVES, n, 3, half, wide), f32),
            pltpu.VMEM((HALVES, n, 3, half, wide), f32),
            dma((2, ch)),
            dma((4,)),
            dma((ITERS - 1, HALVES)),
            dma((ITERS - 1, HALVES, CORES)),
            dma((ITERS - 1, HALVES, CORES)),
            dma((ITERS - 1, HALVES)),
            dma((HALVES,)),
            dma((HALVES,)),
            dma((HALVES,)),
            dma((HALVES,)),
        ],
        compiler_params=pltpu.CompilerParams(
            collective_id=0, has_side_effects=True, vmem_limit_bytes=55184 * 2**10
        ),
        cost_estimate=pl.CostEstimate(flops=2 * 48 * 16 * 256 * 256 * 3, bytes_accessed=4 * 2**20, transcendentals=0),
    )(
        visibility.reshape(ch, 2, rows, wide),
        model.reshape(ch, 2, rows, wide),
        gains_init.reshape(ch, 2, gains_init.shape[3]),
        antenna_mask,
    )
    return gains.reshape(ch, 1, 2, wide)


def solution(mesh):
    n = mesh.shape["col"]
    assert mesh.shape["row"] == n and mesh.shape["chan"] % CORES == 0
    return jax.shard_map(
        functools.partial(per_device, n),
        mesh=mesh,
        in_specs=(
            P("chan", None, None, "row", "col"),
            P("chan", None, None, "row", "col"),
            P("chan", None, None, None),
            P("chan", None),
        ),
        out_specs=P("chan", None, None, "row"),
        check_vma=False,
    )
```

```python
import functools

import jax
import jax.numpy as jnp
from jax import lax
from jax.experimental import pallas as pl
from jax.experimental.pallas import tpu as pltpu
from jax.sharding import PartitionSpec as P

ITERS = 3
HALVES = 2
CORES = 2
DIRECT = ITERS - 2
MESH = pl.DeviceIdType.MESH
SHRINK = 2.0**-5
HUGE = 2.0**60
HUGE_SHRINK = 2.0**-65
DEN_LOWER = 2.0**-4
HUGE_GROW = 2.0**126
NUM_LOWER = SHRINK * DEN_LOWER
LEAST = SHRINK * NUM_LOWER
CHUNK = 64
FIRST = 3


def split(x):
    high = x.astype(jnp.bfloat16).astype(jnp.float32)
    return high, x - high


def stack_bf16(x):
    return jnp.concatenate(split(x), axis=0).astype(jnp.bfloat16)


def dot(x, y, side):
    return lax.dot_general(x, y, (((1,), (side,)), ((), ())), preferred_element_type=jnp.float32)


def farthest_first(n):
    return sorted(range(1, n), key=lambda step: -min(step, n - step))


def nearest_to_zero(n):
    return sorted(range(n), key=lambda place: (min(place, n - place), -place))


def kernel(
    n, vis, mod, gin, mask, out,
    vbuf, mbuf, abuf, bbuf, aflip, bflip, weight, gcol, grow, mcol, mrow, old,
    mine, sums, fresh, arrived, last, direct,
    in_sem, small_sem, sum_send, sum_recv, x_send, x_recv, last_send, last_recv, direct_send, direct_recv,
):
    chan = lax.axis_index("chan")
    row = lax.axis_index("row")
    col = lax.axis_index("col")
    ch, wide = mcol.shape
    half = ch // HALVES
    core = lax.rem(chan, CORES)
    upper = chan - core + 1
    diag = row == col
    owner = jnp.logical_and(diag, core == 1)
    other = jnp.logical_not(owner)
    alone = jnp.logical_and(row == 0, col == 0)
    distant = 1 - alone.astype(jnp.int32)
    column_owner = {"chan": upper, "row": col, "col": col}
    row_owner = {"chan": upper, "row": row, "col": row}

    def loads(k):
        return (
            pltpu.make_async_copy(vis.at[k], vbuf.at[k], in_sem.at[0, k]),
            pltpu.make_async_copy(mod.at[k], mbuf.at[k], in_sem.at[1, k]),
        )

    row_at = pl.ds(pl.multiple_of(row * wide, wide), wide)
    col_at = pl.ds(pl.multiple_of(col * wide, wide), wide)
    small = (
        pltpu.make_async_copy(gin.at[:, :, col_at], gcol, small_sem.at[0]),
        pltpu.make_async_copy(mask.at[:, col_at], mcol, small_sem.at[1]),
        pltpu.make_async_copy(mask.at[:, row_at], mrow, small_sem.at[2]),
        pltpu.make_async_copy(gin.at[:, :, row_at], grow, small_sem.at[3]),
    )
    barrier = pltpu.get_barrier_semaphore()

    def greet(peer):
        pl.semaphore_signal(barrier, inc=1, device_id=peer, device_id_type=MESH)

    @pl.when(owner)
    def _():
        for step in farthest_first(n) + [0]:
            for part in range(CORES):
                if part == 0 or step != 0:
                    greet({"chan": upper - 1 + part, "col": lax.rem(col + step, n)})

    @pl.when(row == 0)
    def _():
        for peer in range(n):
            pl.when(jnp.logical_or(col != 0, peer != 0))(lambda: greet({"row": col, "col": peer}))

    for k in range(ch):
        for copy in loads(k):
            copy.start(priority=int(k >= FIRST))
        if k == 0:
            for copy in small:
                copy.start()
            pl.when(other)(lambda: greet(column_owner))

    row_ids = lax.broadcasted_iota(jnp.int32, weight.shape, 0) + row * wide
    col_ids = lax.broadcasted_iota(jnp.int32, weight.shape, 1) + col * wide
    weight[...] = jnp.where(row_ids == col_ids, 0.0, SHRINK).astype(jnp.bfloat16)

    group = [slice(h * half, (h + 1) * half) for h in range(HALVES)]
    slot = lax.rem(lax.broadcasted_iota(jnp.int32, (2 * half, wide), 0), half)

    def prepare(k):
        for at in range(0, wide, CHUNK):
            rows = pl.ds(at, CHUNK)
            scale = weight[rows]
            m_re = (mbuf[k, 0, rows] * scale).astype(jnp.float32)
            m_im = (mbuf[k, 1, rows] * scale).astype(jnp.float32)
            v_re = vbuf[k, 0, rows].astype(jnp.float32)
            v_im = vbuf[k, 1, rows].astype(jnp.float32)
            values = (m_re * v_re + m_im * v_im, m_re * v_im - m_im * v_re, m_re * m_re + m_im * m_im)
            for place, value in enumerate(values):
                high = value.astype(jnp.bfloat16)
                low = (value - high.astype(jnp.float32)).astype(jnp.bfloat16)
                into, at_lane = (abuf, 2 * place * wide) if place < 2 else (bbuf, 0)
                into[k, rows, at_lane:at_lane + wide] = high
                into[k, rows, at_lane + wide:at_lane + 2 * wide] = low

    def flip():
        @pl.loop(0, ch)
        def _(k):
            for source, target in ((abuf, aflip), (bbuf, bflip)):
                for at in range(0, source.shape[2], wide):
                    target[k, at:at + wide, :] = source[k, :, at:at + wide].T

    def factors(x_re, x_im):
        by_re = stack_bf16(jnp.concatenate([x_re, x_im], axis=0))
        by_im = stack_bf16(jnp.concatenate([-x_im, x_re], axis=0))
        huge = jnp.maximum(jnp.abs(x_re), jnp.abs(x_im)) > HUGE
        down = jnp.where(huge, HUGE_SHRINK, 1.0)
        square = (x_re * down) * (x_re * down) + (x_im * down) * (x_im * down)
        by_b = stack_bf16(jnp.concatenate([jnp.where(huge, 0.0, square), jnp.where(huge, square, 0.0)], axis=0))
        return jnp.concatenate([by_re, by_re, by_im, by_im], axis=1), jnp.concatenate([by_b, by_b], axis=1)

    def add_channel(totals, by, k, flipped):
        num, den = totals
        a, b, side = (aflip, bflip, 0) if flipped else (abuf, bbuf, 1)
        new_num = dot(by[0], a[k], side)
        new_den = dot(by[1], b[k], side)
        here = slot == k % half
        num = jnp.where(here, new_num[0:2 * half] + new_num[2 * half:4 * half], num)
        den = jnp.where(here, new_den[0:2 * half] + new_den[2 * half:4 * half], den)
        return num, den

    def keep(totals, ref):
        num, den = totals
        ref[0] = num[0:half] * NUM_LOWER
        ref[1] = num[half:2 * half] * NUM_LOWER
        ref[2] = den[0:half] * DEN_LOWER + den[half:2 * half] * HUGE_GROW

    def nothing():
        return (jnp.zeros((2 * half, wide), jnp.float32),) * 2

    def quotient(parts):
        total = [parts[0][place] for place in range(3)]
        for part in parts[1:]:
            for place in range(3):
                total[place] = total[place] + part[place]
        least = jnp.maximum(total[2], LEAST)
        return total[0] / least, total[1] / least

    def wait_bytes(ref, sem):
        pltpu.make_async_copy(ref, ref, sem).wait()

    def deliver(it, h, totals):
        if it == ITERS - 1:
            keep(totals, last.at[h, col])
            for peer in nearest_to_zero(n):
                pl.when(col != peer)(pltpu.make_async_remote_copy(
                    src_ref=last.at[h, col], dst_ref=last.at[h, col],
                    send_sem=last_send.at[h], recv_sem=last_recv.at[h],
                    device_id={"col": peer}, device_id_type=MESH,
                ).start)
            return

        if it == DIRECT:
            keep(totals, mine.at[it, h])
            pl.when(alone)(lambda: keep(totals, direct.at[h, col]))
            pl.when(jnp.logical_not(alone))(pltpu.make_async_remote_copy(
                src_ref=mine.at[it, h], dst_ref=direct.at[h, col],
                send_sem=direct_send.at[h], recv_sem=direct_recv.at[h],
                device_id={"row": 0, "col": row}, device_id_type=MESH,
            ).start)

        @pl.when(owner)
        def _():
            keep(totals, sums.at[it, h, 1, col])

        @pl.when(other)
        def _():
            if it != DIRECT:
                keep(totals, mine.at[it, h])
            pltpu.make_async_remote_copy(
                src_ref=mine.at[it, h], dst_ref=sums.at[it, h, core, col],
                send_sem=sum_send.at[it, h], recv_sem=sum_recv.at[it, h, core],
                device_id=row_owner, device_id_type=MESH,
            ).start()

    def settle(it, h, part):
        wait_bytes(sums.at[it, h, part, 0:n - part], sum_recv.at[it, h, part])
        re, im = quotient([sums.at[it, h, part, peer] for peer in range(n)])
        fresh[it, h, part, 0] = re
        fresh[it, h, part, 1] = im
        if part == 1:
            arrived[it, h, 0] = re
            arrived[it, h, 1] = im
        def send_to(peer):
            pltpu.make_async_remote_copy(
                src_ref=fresh.at[it, h, part], dst_ref=arrived.at[it, h],
                send_sem=x_send.at[it, h, part], recv_sem=x_recv.at[it, h],
                device_id={"chan": upper - 1 + part, "row": peer}, device_id_type=MESH,
            ).start()

        if it == DIRECT:
            for peer in range(1, n):
                if part == 0:
                    send_to(peer)
                else:
                    pl.when(row != peer)(lambda: send_to(peer))
        else:
            for step in farthest_first(n) + [0] * (part == 0):
                send_to(lax.rem(row + step, n))

    def first_factors(h):
        usable = mcol[group[h], :] > 0
        x = [jnp.where(usable, gcol[group[h], part, :], 0.0) for part in range(2)]
        return factors(*x)

    totals = nothing()
    ready = 0
    for k in range(ch + 1):
        if k == ready < ch:
            until = FIRST if k == 0 else ch
            for arrival in range(k, until):
                for copy in loads(arrival):
                    copy.wait()
            ready = until
        if k == 1:
            for copy in small:
                copy.wait()
            by = [first_factors(h) for h in range(HALVES)]
        if k > 0:
            totals = add_channel(totals, by[(k - 1) // half], k - 1, False)
        if k < ch:
            prepare(k)
        if k > 0 and k % half == 0:
            if k == half:
                pl.when(other)(lambda: pl.semaphore_wait(barrier, 1 + distant))
            deliver(0, k // half - 1, totals)
            totals = nothing()

    for it in range(ITERS - 1):
        @pl.when(owner)
        def _():
            if it == 0:
                pl.semaphore_wait(barrier, CORES * n - 1 + distant)
            for h in range(HALVES):
                for part in (1, 0):
                    settle(it, h, part)

        if it == 0:
            flip()
        for h in range(HALVES):
            if it == DIRECT:
                @pl.when(row == 0)
                def _():
                    pl.when(col == 0)(lambda: wait_bytes(direct.at[h, 0:n - 1], direct_recv.at[h]))
                    pl.when(col != 0)(lambda: wait_bytes(direct.at[h], direct_recv.at[h]))
                    for part, value in enumerate(quotient([direct.at[h, peer] for peer in range(n)])):
                        arrived[it, h, part] = value

                pl.when(jnp.logical_and(other, row != 0))(lambda: wait_bytes(arrived.at[it, h], x_recv.at[it, h]))
            else:
                pl.when(other)(lambda: wait_bytes(arrived.at[it, h], x_recv.at[it, h]))
            usable = mcol[group[h], :] > 0
            x = []
            for part in range(2):
                value = arrived[it, h, part]
                if it % 2 == 1:
                    value = 0.5 * (value + old[h, part])
                elif it + 1 < ITERS - 1:
                    old[h, part] = value
                x.append(jnp.where(usable, value, 0.0))
            by = factors(*x)
            totals = nothing()
            for k in range(h * half, (h + 1) * half):
                totals = add_channel(totals, by, k, True)
            deliver(it + 1, h, totals)

    for h in range(HALVES):
        wait_bytes(last.at[h, 0:n - 1], last_recv.at[h])
        usable = mrow[group[h], :] > 0
        for part, value in enumerate(quotient([last.at[h, peer] for peer in range(n)])):
            out[group[h], part, :] = jnp.where(usable, value, grow[group[h], part, :])

    for it in range(ITERS - 1):
        for h in range(HALVES):
            pl.when(other)(lambda: wait_bytes(mine.at[it, h], sum_send.at[it, h]))

            @pl.when(owner)
            def _():
                if it == DIRECT:
                    wait_bytes(sums.at[0, 0, 0, 0:n - 1, 0:2], x_send.at[it, h, 0])
                    pl.when(row == 0)(lambda: wait_bytes(sums.at[0, 0, 0, 0:n - 1, 0:2], x_send.at[it, h, 1]))
                    if n > 2:
                        pl.when(row != 0)(lambda: wait_bytes(sums.at[0, 0, 0, 0:n - 2, 0:2], x_send.at[it, h, 1]))
                else:
                    for part in range(CORES):
                        wait_bytes(sums.at[0, 0, 0, 0:n - part, 0:2], x_send.at[it, h, part])
    for h in range(HALVES):
        pl.when(jnp.logical_or(row != 0, col != 0))(lambda: wait_bytes(mine.at[0, h], direct_send.at[h]))
        wait_bytes(last.at[h, 0:n - 1], last_send.at[h])


def per_device(n, visibility, model, gains_init, antenna_mask):
    assert ITERS == 3
    ch, _, _, rows, wide = visibility.shape
    half = ch // HALVES
    f32, bf16 = jnp.float32, jnp.bfloat16
    hbm = pl.BlockSpec(memory_space=pltpu.HBM)
    dma = pltpu.SemaphoreType.DMA
    gains = pl.pallas_call(
        functools.partial(kernel, n),
        out_shape=jax.ShapeDtypeStruct((ch, 2, wide), f32),
        in_specs=[hbm] * 4,
        out_specs=pl.BlockSpec(memory_space=pltpu.VMEM),
        scratch_shapes=[
            pltpu.VMEM((ch, 2, rows, wide), bf16),
            pltpu.VMEM((ch, 2, rows, wide), bf16),
            pltpu.VMEM((ch, rows, 4 * wide), bf16),
            pltpu.VMEM((ch, rows, 2 * wide), bf16),
            pltpu.VMEM((ch, 4 * wide, rows), bf16),
            pltpu.VMEM((ch, 2 * wide, rows), bf16),
            pltpu.VMEM((rows, wide), bf16),
            pltpu.VMEM((ch, 2, wide), f32),
            pltpu.VMEM((ch, 2, wide), f32),
            pltpu.VMEM((ch, wide), jnp.int32),
            pltpu.VMEM((ch, wide), jnp.int32),
            pltpu.VMEM((HALVES, 2, half, wide), f32),
            pltpu.VMEM((ITERS - 1, HALVES, 3, half, wide), f32),
            pltpu.VMEM((ITERS - 1, HALVES, CORES, n, 3, half, wide), f32),
            pltpu.VMEM((ITERS - 1, HALVES, CORES, 2, half, wide), f32),
            pltpu.VMEM((ITERS - 1, HALVES, 2, half, wide), f32),
            pltpu.VMEM((HALVES, n, 3, half, wide), f32),
            pltpu.VMEM((HALVES, n, 3, half, wide), f32),
            dma((2, ch)),
            dma((4,)),
            dma((ITERS - 1, HALVES)),
            dma((ITERS - 1, HALVES, CORES)),
            dma((ITERS - 1, HALVES, CORES)),
            dma((ITERS - 1, HALVES)),
            dma((HALVES,)),
            dma((HALVES,)),
            dma((HALVES,)),
            dma((HALVES,)),
        ],
        compiler_params=pltpu.CompilerParams(
            collective_id=0, has_side_effects=True, vmem_limit_bytes=55184 * 2**10
        ),
        cost_estimate=pl.CostEstimate(flops=2 * 48 * 16 * 256 * 256 * 3, bytes_accessed=4 * 2**20, transcendentals=0),
    )(
        visibility.reshape(ch, 2, rows, wide),
        model.reshape(ch, 2, rows, wide),
        gains_init.reshape(ch, 2, gains_init.shape[3]),
        antenna_mask,
    )
    return gains.reshape(ch, 1, 2, wide)


def solution(mesh):
    n = mesh.shape["col"]
    assert mesh.shape["row"] == n and mesh.shape["chan"] % CORES == 0
    return jax.shard_map(
        functools.partial(per_device, n),
        mesh=mesh,
        in_specs=(
            P("chan", None, None, "row", "col"),
            P("chan", None, None, "row", "col"),
            P("chan", None, None, None),
            P("chan", None),
        ),
        out_specs=P("chan", None, None, "row"),
        check_vma=False,
    )
```

```python
import functools

import jax
import jax.numpy as jnp
from jax import lax
from jax.experimental import pallas as pl
from jax.experimental.pallas import tpu as pltpu
from jax.sharding import PartitionSpec as P

ITERS = 3
HALVES = 2
CORES = 2
DIRECT = ITERS - 2
MESH = pl.DeviceIdType.MESH
SHRINK = 2.0**-5
HUGE = 2.0**60
HUGE_SHRINK = 2.0**-65
DEN_LOWER = 2.0**-4
HUGE_GROW = 2.0**126
NUM_LOWER = SHRINK * DEN_LOWER
LEAST = SHRINK * NUM_LOWER
CHUNK = 64
FIRST = 3


def split(x):
    high = x.astype(jnp.bfloat16).astype(jnp.float32)
    return high, x - high


def stack_bf16(x):
    return jnp.concatenate(split(x), axis=0).astype(jnp.bfloat16)


def dot(x, y, side):
    return lax.dot_general(x, y, (((1,), (side,)), ((), ())), preferred_element_type=jnp.float32)


def farthest_first(n):
    return sorted(range(1, n), key=lambda step: -min(step, n - step))


def nearest_to_zero(n):
    return sorted(range(n), key=lambda place: (min(place, n - place), -place))


def kernel(
    n, vis, mod, gin, mask, out,
    vbuf, mbuf, abuf, bbuf, aflip, bflip, weight, gcol, grow, mcol, mrow, old,
    mine, sums, fresh, arrived, last, direct,
    in_sem, small_sem, sum_send, sum_recv, x_send, x_recv, last_send, last_recv, direct_send, direct_recv,
):
    chan = lax.axis_index("chan")
    row = lax.axis_index("row")
    col = lax.axis_index("col")
    ch, wide = mcol.shape
    half = ch // HALVES
    core = lax.rem(chan, CORES)
    upper = chan - core + 1
    diag = row == col
    owner = jnp.logical_and(diag, core == 1)
    other = jnp.logical_not(owner)
    alone = jnp.logical_and(row == 0, col == 0)
    distant = 1 - alone.astype(jnp.int32)
    column_owner = {"chan": upper, "row": col, "col": col}
    row_owner = {"chan": upper, "row": row, "col": row}

    def loads(k):
        return (
            pltpu.make_async_copy(vis.at[k], vbuf.at[k], in_sem.at[0, k]),
            pltpu.make_async_copy(mod.at[k], mbuf.at[k], in_sem.at[1, k]),
        )

    row_at = pl.ds(pl.multiple_of(row * wide, wide), wide)
    col_at = pl.ds(pl.multiple_of(col * wide, wide), wide)
    small = (
        pltpu.make_async_copy(gin.at[:, :, col_at], gcol, small_sem.at[0]),
        pltpu.make_async_copy(mask.at[:, col_at], mcol, small_sem.at[1]),
        pltpu.make_async_copy(mask.at[:, row_at], mrow, small_sem.at[2]),
        pltpu.make_async_copy(gin.at[:, :, row_at], grow, small_sem.at[3]),
    )
    barrier = pltpu.get_barrier_semaphore()

    def greet(peer):
        pl.semaphore_signal(barrier, inc=1, device_id=peer, device_id_type=MESH)

    @pl.when(owner)
    def _():
        for step in farthest_first(n) + [0]:
            for part in range(CORES):
                if part == 0 or step != 0:
                    greet({"chan": upper - 1 + part, "col": lax.rem(col + step, n)})

    @pl.when(row == 0)
    def _():
        for peer in range(n):
            pl.when(jnp.logical_or(col != 0, peer != 0))(lambda: greet({"row": col, "col": peer}))

    for k in range(ch):
        for copy in loads(k):
            copy.start(priority=int(k >= FIRST))
        if k == 0:
            for copy in small:
                copy.start()
            pl.when(other)(lambda: greet(column_owner))

    row_ids = lax.broadcasted_iota(jnp.int32, weight.shape, 0) + row * wide
    col_ids = lax.broadcasted_iota(jnp.int32, weight.shape, 1) + col * wide
    weight[...] = jnp.where(row_ids == col_ids, 0.0, SHRINK).astype(jnp.bfloat16)

    group = [slice(h * half, (h + 1) * half) for h in range(HALVES)]
    slot = lax.rem(lax.broadcasted_iota(jnp.int32, (2 * half, wide), 0), half)

    def prepare(k):
        for at in range(0, wide, CHUNK):
            rows = pl.ds(at, CHUNK)
            scale = weight[rows]
            m_re = (mbuf[k, 0, rows] * scale).astype(jnp.float32)
            m_im = (mbuf[k, 1, rows] * scale).astype(jnp.float32)
            v_re = vbuf[k, 0, rows].astype(jnp.float32)
            v_im = vbuf[k, 1, rows].astype(jnp.float32)
            values = (m_re * v_re + m_im * v_im, m_re * v_im - m_im * v_re, m_re * m_re + m_im * m_im)
            for place, value in enumerate(values):
                high = value.astype(jnp.bfloat16)
                low = (value - high.astype(jnp.float32)).astype(jnp.bfloat16)
                into, at_lane = (abuf, 2 * place * wide) if place < 2 else (bbuf, 0)
                into[k, rows, at_lane:at_lane + wide] = high
                into[k, rows, at_lane + wide:at_lane + 2 * wide] = low

    def flip():
        @pl.loop(0, ch)
        def _(k):
            for source, target in ((abuf, aflip), (bbuf, bflip)):
                for at in range(0, source.shape[2], wide):
                    target[k, at:at + wide, :] = source[k, :, at:at + wide].T

    def factors(x_re, x_im):
        by_re = stack_bf16(jnp.concatenate([x_re, x_im], axis=0))
        by_im = stack_bf16(jnp.concatenate([-x_im, x_re], axis=0))
        huge = jnp.maximum(jnp.abs(x_re), jnp.abs(x_im)) > HUGE
        down = jnp.where(huge, HUGE_SHRINK, 1.0)
        square = (x_re * down) * (x_re * down) + (x_im * down) * (x_im * down)
        by_b = stack_bf16(jnp.concatenate([jnp.where(huge, 0.0, square), jnp.where(huge, square, 0.0)], axis=0))
        return jnp.concatenate([by_re, by_re, by_im, by_im], axis=1), jnp.concatenate([by_b, by_b], axis=1)

    def add_channel(totals, by, k, flipped):
        num, den = totals
        a, b, side = (aflip, bflip, 0) if flipped else (abuf, bbuf, 1)
        new_num = dot(by[0], a[k], side)
        new_den = dot(by[1], b[k], side)
        here = slot == k % half
        num = jnp.where(here, new_num[0:2 * half] + new_num[2 * half:4 * half], num)
        den = jnp.where(here, new_den[0:2 * half] + new_den[2 * half:4 * half], den)
        return num, den

    def keep(totals, ref):
        num, den = totals
        ref[0] = num[0:half] * NUM_LOWER
        ref[1] = num[half:2 * half] * NUM_LOWER
        ref[2] = den[0:half] * DEN_LOWER + den[half:2 * half] * HUGE_GROW

    def nothing():
        return (jnp.zeros((2 * half, wide), jnp.float32),) * 2

    def quotient(parts):
        total = [[part[place] for part in parts] for place in range(3)]
        while len(total[0]) > 1:
            total = [[one + two for one, two in zip(terms[::2], terms[1::2])] for terms in total]
        scale = 1.0 / jnp.maximum(total[2][0], LEAST)
        return total[0][0] * scale, total[1][0] * scale

    def wait_bytes(ref, sem):
        pltpu.make_async_copy(ref, ref, sem).wait()

    def deliver(it, h, totals):
        if it == ITERS - 1:
            keep(totals, last.at[h, col])
            for peer in nearest_to_zero(n):
                pl.when(col != peer)(pltpu.make_async_remote_copy(
                    src_ref=last.at[h, col], dst_ref=last.at[h, col],
                    send_sem=last_send.at[h], recv_sem=last_recv.at[h],
                    device_id={"col": peer}, device_id_type=MESH,
                ).start)
            return

        if it == DIRECT:
            keep(totals, mine.at[it, h])
            pl.when(alone)(lambda: keep(totals, direct.at[h, col]))
            pl.when(jnp.logical_not(alone))(pltpu.make_async_remote_copy(
                src_ref=mine.at[it, h], dst_ref=direct.at[h, col],
                send_sem=direct_send.at[h], recv_sem=direct_recv.at[h],
                device_id={"row": 0, "col": row}, device_id_type=MESH,
            ).start)

        @pl.when(owner)
        def _():
            keep(totals, sums.at[it, h, 1, col])

        @pl.when(other)
        def _():
            if it != DIRECT:
                keep(totals, mine.at[it, h])
            pltpu.make_async_remote_copy(
                src_ref=mine.at[it, h], dst_ref=sums.at[it, h, core, col],
                send_sem=sum_send.at[it, h], recv_sem=sum_recv.at[it, h, core],
                device_id=row_owner, device_id_type=MESH,
            ).start()

    def settle(it, h, part):
        wait_bytes(sums.at[it, h, part, 0:n - part], sum_recv.at[it, h, part])
        re, im = quotient([sums.at[it, h, part, peer] for peer in range(n)])
        fresh[it, h, part, 0] = re
        fresh[it, h, part, 1] = im
        if part == 1:
            arrived[it, h, 0] = re
            arrived[it, h, 1] = im
        def send_to(peer):
            pltpu.make_async_remote_copy(
                src_ref=fresh.at[it, h, part], dst_ref=arrived.at[it, h],
                send_sem=x_send.at[it, h, part], recv_sem=x_recv.at[it, h],
                device_id={"chan": upper - 1 + part, "row": peer}, device_id_type=MESH,
            ).start()

        if it == DIRECT:
            for peer in range(1, n):
                if part == 0:
                    send_to(peer)
                else:
                    pl.when(row != peer)(lambda: send_to(peer))
        else:
            for step in farthest_first(n) + [0] * (part == 0):
                send_to(lax.rem(row + step, n))

    def first_factors(h):
        usable = mcol[group[h], :] > 0
        x = [jnp.where(usable, gcol[group[h], part, :], 0.0) for part in range(2)]
        return factors(*x)

    totals = nothing()
    ready = 0
    for k in range(ch + 1):
        if k == ready < ch:
            until = FIRST if k == 0 else ch
            for arrival in range(k, until):
                for copy in loads(arrival):
                    copy.wait()
            ready = until
        if k == 1:
            for copy in small:
                copy.wait()
            by = [first_factors(h) for h in range(HALVES)]
        if k > 0:
            totals = add_channel(totals, by[(k - 1) // half], k - 1, False)
        if k < ch:
            prepare(k)
        if k > 0 and k % half == 0:
            if k == half:
                pl.when(other)(lambda: pl.semaphore_wait(barrier, 1 + distant))
            deliver(0, k // half - 1, totals)
            totals = nothing()

    for it in range(ITERS - 1):
        @pl.when(owner)
        def _():
            if it == 0:
                pl.semaphore_wait(barrier, CORES * n - 1 + distant)
            for h in range(HALVES):
                for part in (1, 0):
                    settle(it, h, part)

        if it == 0:
            flip()
        for h in range(HALVES):
            if it == DIRECT:
                @pl.when(row == 0)
                def _():
                    pl.when(col == 0)(lambda: wait_bytes(direct.at[h, 0:n - 1], direct_recv.at[h]))
                    pl.when(col != 0)(lambda: wait_bytes(direct.at[h], direct_recv.at[h]))
                    for part, value in enumerate(quotient([direct.at[h, peer] for peer in range(n)])):
                        arrived[it, h, part] = value

                pl.when(jnp.logical_and(other, row != 0))(lambda: wait_bytes(arrived.at[it, h], x_recv.at[it, h]))
            else:
                pl.when(other)(lambda: wait_bytes(arrived.at[it, h], x_recv.at[it, h]))
            usable = mcol[group[h], :] > 0
            x = []
            for part in range(2):
                value = arrived[it, h, part]
                if it % 2 == 1:
                    value = 0.5 * (value + old[h, part])
                elif it + 1 < ITERS - 1:
                    old[h, part] = value
                x.append(jnp.where(usable, value, 0.0))
            by = factors(*x)
            totals = nothing()
            for k in range(h * half, (h + 1) * half):
                totals = add_channel(totals, by, k, True)
            deliver(it + 1, h, totals)

    for h in range(HALVES):
        wait_bytes(last.at[h, 0:n - 1], last_recv.at[h])
        usable = mrow[group[h], :] > 0
        for part, value in enumerate(quotient([last.at[h, peer] for peer in range(n)])):
            out[group[h], part, :] = jnp.where(usable, value, grow[group[h], part, :])

    for it in range(ITERS - 1):
        for h in range(HALVES):
            pl.when(other)(lambda: wait_bytes(mine.at[it, h], sum_send.at[it, h]))

            @pl.when(owner)
            def _():
                if it == DIRECT:
                    wait_bytes(sums.at[0, 0, 0, 0:n - 1, 0:2], x_send.at[it, h, 0])
                    pl.when(row == 0)(lambda: wait_bytes(sums.at[0, 0, 0, 0:n - 1, 0:2], x_send.at[it, h, 1]))
                    if n > 2:
                        pl.when(row != 0)(lambda: wait_bytes(sums.at[0, 0, 0, 0:n - 2, 0:2], x_send.at[it, h, 1]))
                else:
                    for part in range(CORES):
                        wait_bytes(sums.at[0, 0, 0, 0:n - part, 0:2], x_send.at[it, h, part])
    for h in range(HALVES):
        pl.when(jnp.logical_or(row != 0, col != 0))(lambda: wait_bytes(mine.at[0, h], direct_send.at[h]))
        wait_bytes(last.at[h, 0:n - 1], last_send.at[h])


def per_device(n, visibility, model, gains_init, antenna_mask):
    assert ITERS == 3
    ch, _, _, rows, wide = visibility.shape
    half = ch // HALVES
    f32, bf16 = jnp.float32, jnp.bfloat16
    hbm = pl.BlockSpec(memory_space=pltpu.HBM)
    dma = pltpu.SemaphoreType.DMA
    gains = pl.pallas_call(
        functools.partial(kernel, n),
        out_shape=jax.ShapeDtypeStruct((ch, 2, wide), f32),
        in_specs=[hbm] * 4,
        out_specs=pl.BlockSpec(memory_space=pltpu.VMEM),
        scratch_shapes=[
            pltpu.VMEM((ch, 2, rows, wide), bf16),
            pltpu.VMEM((ch, 2, rows, wide), bf16),
            pltpu.VMEM((ch, rows, 4 * wide), bf16),
            pltpu.VMEM((ch, rows, 2 * wide), bf16),
            pltpu.VMEM((ch, 4 * wide, rows), bf16),
            pltpu.VMEM((ch, 2 * wide, rows), bf16),
            pltpu.VMEM((rows, wide), bf16),
            pltpu.VMEM((ch, 2, wide), f32),
            pltpu.VMEM((ch, 2, wide), f32),
            pltpu.VMEM((ch, wide), jnp.int32),
            pltpu.VMEM((ch, wide), jnp.int32),
            pltpu.VMEM((HALVES, 2, half, wide), f32),
            pltpu.VMEM((ITERS - 1, HALVES, 3, half, wide), f32),
            pltpu.VMEM((ITERS - 1, HALVES, CORES, n, 3, half, wide), f32),
            pltpu.VMEM((ITERS - 1, HALVES, CORES, 2, half, wide), f32),
            pltpu.VMEM((ITERS - 1, HALVES, 2, half, wide), f32),
            pltpu.VMEM((HALVES, n, 3, half, wide), f32),
            pltpu.VMEM((HALVES, n, 3, half, wide), f32),
            dma((2, ch)),
            dma((4,)),
            dma((ITERS - 1, HALVES)),
            dma((ITERS - 1, HALVES, CORES)),
            dma((ITERS - 1, HALVES, CORES)),
            dma((ITERS - 1, HALVES)),
            dma((HALVES,)),
            dma((HALVES,)),
            dma((HALVES,)),
            dma((HALVES,)),
        ],
        compiler_params=pltpu.CompilerParams(
            collective_id=0, has_side_effects=True, vmem_limit_bytes=55184 * 2**10
        ),
        cost_estimate=pl.CostEstimate(flops=2 * 48 * 16 * 256 * 256 * 3, bytes_accessed=4 * 2**20, transcendentals=0),
    )(
        visibility.reshape(ch, 2, rows, wide),
        model.reshape(ch, 2, rows, wide),
        gains_init.reshape(ch, 2, gains_init.shape[3]),
        antenna_mask,
    )
    return gains.reshape(ch, 1, 2, wide)


def solution(mesh):
    n = mesh.shape["col"]
    assert mesh.shape["row"] == n and mesh.shape["chan"] % CORES == 0
    return jax.shard_map(
        functools.partial(per_device, n),
        mesh=mesh,
        in_specs=(
            P("chan", None, None, "row", "col"),
            P("chan", None, None, "row", "col"),
            P("chan", None, None, None),
            P("chan", None),
        ),
        out_specs=P("chan", None, None, "row"),
        check_vma=False,
    )
```
